32 devices in a mesh: prow: 4 (over y, core), pcol: 8 (over z, x).
Axes of the slice: x: 2, y: 2, z: 4, core: 2. Of those that a mesh axis runs over, the one named last changes fastest.
Arguments:
- ainv: bfloat16 [4096, 4096], P('pcol', 'prow'), may hold values from -6 to 6
- lpanel: bfloat16 [4096, 2048], P('prow', 'pcol'), may hold values from -0.125 to 0.125
- dinv: float32 [256, 2048], P(None, 'prow'), may hold values from -6 to 6
- rowblocks: int32 [8, 10], replicated, may hold values from 0 to 15, as said below
- counts: int32 [8], replicated, may hold values from 7 to 10
- widths: int32 [8], replicated, may hold values from 1 to 256, 1536 in all
Outputs:
- selected_inverse: bfloat16 [4096, 2048], P('pcol', 'prow')
- diagonal_blocks: float32 [256, 2048], P(None, 'prow')
The draws below stay inside these ranges and needn't reach their ends.
Inputs may be any that keep to these rules, and one draw needn't show every extreme that they name: The entries of one row of rowblocks are distinct; only the first counts[k] entries of row k belong to supernode k. The widths sum to 1536.
All inputs are finite; a program needn't handle non-finite values.
Results may differ from the reference program's by a relative error of at most 0.02.
Values may be sent and summed in bfloat16 or wider, within the bound.
A program may use at most 64 MiB of HBM per device.

```python
import math
import jax
import jax.numpy as jnp
import numpy as np
from jax import lax

B = 256
SNODES = 8
NB = 16
RB = 4
SMAX = 10
N_PROW = 4


def draw_rowblocks(key, part):
    key = jax.random.fold_in(key, 11)
    node_keys = jax.random.split(key, SNODES)
    orders = jax.vmap(lambda single: jax.random.permutation(single, NB))(node_keys)
    return orders[:, :SMAX].astype(jnp.int32)


def draw_counts(key, part):
    key = jax.random.fold_in(key, 23)
    count_key, slot_key, other_key = jax.random.split(key, 3)
    fewest = 3 * SMAX // 4
    values = jax.random.randint(count_key, (SNODES,), fewest, SMAX + 1)
    target_slot = jax.random.randint(slot_key, (), 0, SNODES)
    other_slot = (target_slot + 1 + jax.random.randint(other_key, (), 0, SNODES - 1)) % SNODES
    values = values.at[target_slot].set(SMAX)
    values = values.at[other_slot].set(fewest)
    return values.astype(jnp.int32)


def steps_of(own_key, shape, pieces, smallest, largest):
    def one(position, parts):
        heights = jax.random.uniform(jax.random.fold_in(jax.random.fold_in(own_key, 6), position), (parts,), jnp.float32, smallest / len(pieces), largest / len(pieces))
        return jnp.repeat(jnp.exp(heights), shape[position] // parts).reshape((-1,) + (1,) * (len(shape) - position - 1))

    factor_of = one(*pieces[0])
    for cut in pieces[1:]:
        factor_of = factor_of * one(*cut)
    return factor_of


def profile(amount, total, most, slope):
    portions = [(1 << 20) // math.isqrt(grade ** slope) + 1 for grade in range(2, amount + 1)]
    rest, holding = total - most - (amount - 1), [1] * (amount - 1)
    while rest > 0:
        candidates = [i for i in range(amount - 1) if holding[i] < most]
        whole, remaining = sum([portions[i] for i in candidates]), rest
        for i in candidates:
            extra = min(most - holding[i], max(1, remaining * portions[i] // whole), rest)
            holding[i] = holding[i] + extra
            rest = rest - extra
    return np.array([most] + holding)


def ragged_sizes(own_key, number_of, total, reach, slope):
    if number_of == 2:
        one = jax.random.randint(own_key, (), max(1, total - reach), min(reach, total - 1) + 1)
        return jnp.stack([one, total - one])
    sizes = jnp.asarray(profile(number_of, total, reach, slope), jnp.int32)
    pairs = (number_of - 1) // 2
    donor, taker = sizes[1:1 + 2 * pairs:2], sizes[2:2 + 2 * pairs:2]
    margin = jnp.minimum(donor - 1, reach - taker)
    moved = jax.random.randint(jax.random.fold_in(own_key, 1), (pairs,), 0, 1 << 20) % (margin + 1)
    sizes = sizes.at[1:1 + 2 * pairs:2].set(donor - moved).at[2:2 + 2 * pairs:2].set(taker + moved)
    return sizes[jax.random.permutation(jax.random.fold_in(own_key, 2), number_of)]


def normal_values(key, extent, spread, reach, pieces=(), held_as=jnp.bfloat16):
    level = steps_of(key, extent, pieces, -0.22, 0.18) if pieces else 1.0
    array = jax.random.normal(key, extent, jnp.float32) * spread * level
    return jnp.minimum(jnp.maximum(array, -reach), reach).astype(held_as)


def setup_inputs(seed: int = 0) -> dict:
    keys = jax.random.split(jax.random.key(seed), 7)
    ainv = normal_values(keys[0], (NB * B, NB * B), 1.0, 6.0, ((0, 8), (1, 4)))
    lpanel = normal_values(keys[1], (NB * B, SNODES * B), (SMAX * B) ** -0.5, 0.125, ((0, 4), (1, 8)))
    dinv = normal_values(keys[2], (B, SNODES * B), 1.0, 6.0, ((1, 4),), jnp.float32)
    rowblocks = draw_rowblocks(jax.random.fold_in(keys[6], 71), 0)
    counts = draw_counts(jax.random.fold_in(keys[6], 71), 0)
    widths = ragged_sizes(keys[5], SNODES, SNODES * B * 3 // 4, B, 2).astype(jnp.int32)
    return dict(ainv=ainv, lpanel=lpanel, dinv=dinv, rowblocks=rowblocks, counts=counts, widths=widths)


def one_supernode(ainv, lpanel, dinv, rowblocks, counts, widths, supernode):
    struct_rows = rowblocks[supernode]
    slot_live = jnp.arange(SMAX, dtype=jnp.int32) < counts[supernode]
    column_live = jnp.arange(B, dtype=jnp.int32) < widths[supernode]
    row_index = (struct_rows[:, None] * B + jnp.arange(B, dtype=jnp.int32)[None, :]).reshape(SMAX * B).astype(jnp.int32)
    first_col = (supernode * B).astype(jnp.int32)
    panel_cols = lax.dynamic_slice_in_dim(lpanel, first_col, B, 1)
    factor = panel_cols[row_index].reshape(SMAX, B, B)
    keep_mask = slot_live[:, None, None] & column_live[None, None, :]
    factor = jnp.where(keep_mask, factor, jnp.zeros((), jnp.bfloat16))
    inverse_rows = ainv[row_index]
    inverse_sub = inverse_rows[:, row_index].reshape(SMAX * B, SMAX, B).astype(jnp.float32)
    factor_wide = factor.astype(jnp.float32)
    products = jnp.einsum("itb,tbc->tic", inverse_sub, factor_wide, precision=lax.Precision.HIGHEST)
    group_rows = struct_rows // RB
    member = ((group_rows[None, :] == jnp.arange(N_PROW, dtype=jnp.int32)[:, None]) & slot_live[None, :]).astype(jnp.float32)
    partials = jnp.einsum("gt,tic->gic", member, products, precision=lax.Precision.HIGHEST)
    rounded = lax.optimization_barrier(partials.astype(jnp.bfloat16)).astype(jnp.float32)
    selected = jnp.sum(rounded, axis=0)
    row_live = jnp.repeat(slot_live, B)[:, None]
    offdiag = jnp.where(row_live, -selected, jnp.zeros((), jnp.float32)).astype(jnp.bfloat16)
    quadratic = jnp.einsum("sbc,sbd->cd", factor_wide, selected.reshape(SMAX, B, B), precision=lax.Precision.HIGHEST)
    corner = column_live[:, None] & column_live[None, :]
    own_inverse = lax.dynamic_slice_in_dim(dinv, first_col, B, 1)
    diagonal = jnp.where(corner, own_inverse, jnp.zeros((), jnp.float32)) + quadratic
    return offdiag, row_index, diagonal


def reference(ainv, lpanel, dinv, rowblocks, counts, widths):
    def visit_node(supernode):
        return one_supernode(ainv, lpanel, dinv, rowblocks, counts, widths, supernode)

    offdiag_parts, row_parts, diagonal_parts = lax.map(visit_node, jnp.arange(SNODES, dtype=jnp.int32))
    column_index = (jnp.arange(SNODES, dtype=jnp.int32)[:, None] * B + jnp.arange(B, dtype=jnp.int32)[None, :]).astype(jnp.int32)
    selected_inverse = jnp.zeros((NB * B, SNODES * B), jnp.bfloat16)
    selected_inverse = selected_inverse.at[row_parts[:, :, None], column_index[:, None, :]].set(offdiag_parts)
    diagonal_blocks = jnp.transpose(diagonal_parts, (1, 0, 2)).reshape(B, SNODES * B)
    return selected_inverse, diagonal_blocks
```

```python
import functools

import jax
import jax.numpy as jnp
from jax import lax
from jax.experimental import pallas as pl
from jax.experimental.pallas import tpu as pltpu
from jax.sharding import PartitionSpec as P

MESH = pl.DeviceIdType.MESH

B = 256
SNODES = 8


def from_root(value, axis, source):
    kept = jnp.where(lax.axis_index(axis) == source, value, 0).astype(value.dtype)
    return lax.psum(kept, axis)


def block_mask(block_ids, column_ids, rowblocks, counts, widths):
    slot_total = rowblocks.shape[1]
    owner_node = column_ids // B
    within = column_ids % B
    chosen = owner_node[:, None] == jnp.arange(SNODES, dtype=jnp.int32)[None, :]
    owner_rows = jnp.sum(jnp.where(chosen[:, :, None], rowblocks[None, :, :], 0), axis=1)
    owner_count = jnp.sum(jnp.where(chosen, counts[None, :], 0), axis=1)
    owner_width = jnp.sum(jnp.where(chosen, widths[None, :], 0), axis=1)
    slot_live = jnp.arange(slot_total, dtype=jnp.int32)[None, :] < owner_count[:, None]
    matched = (owner_rows[None, :, :] == block_ids[:, None, None]) & slot_live[None, :, :]
    present = jnp.any(matched, axis=2) & (within < owner_width)[None, :]
    return (present, owner_width, within)


def per_device(ainv, lpanel, dinv, rowblocks, counts, widths):
    row_group = lax.axis_index("prow")
    col_group = lax.axis_index("pcol")
    panel_rows = lpanel.shape[0]
    panel_cols = lpanel.shape[1]
    inverse_rows = ainv.shape[0]
    share_cols = dinv.shape[1]
    row_blocks = panel_rows // B
    col_blocks = inverse_rows // B
    own_ids = row_group * row_blocks + jnp.arange(row_blocks, dtype=jnp.int32)
    own_cols = col_group * panel_cols + jnp.arange(panel_cols, dtype=jnp.int32)
    present, unused_width, unused_within = block_mask(own_ids, own_cols, rowblocks, counts, widths)
    masked = jnp.where(
        present[:, None, :], lpanel.reshape(row_blocks, B, panel_cols), jnp.zeros((), jnp.bfloat16)
    )
    masked = masked.reshape(panel_rows, panel_cols)
    gathered = lax.all_gather(masked, "pcol", axis=1, tiled=True)
    product = jnp.dot(ainv, gathered, preferred_element_type=jnp.float32)
    root_row = col_group * col_blocks // row_blocks
    offset = (col_group * col_blocks - root_row * row_blocks) * B
    own_rows = lax.dynamic_slice_in_dim(gathered, offset, inverse_rows, 0)
    width_cols = max(share_cols, B)
    first_col = row_group * share_cols // width_cols * width_cols
    summed = lax.psum_scatter(
        product.astype(jnp.bfloat16), "prow", scatter_dimension=1, tiled=True
    ).astype(jnp.float32)
    whole_rows = from_root(own_rows, "prow", root_row)
    across = lax.dynamic_slice_in_dim(whole_rows, first_col, width_cols, 1)
    column_ids = row_group * share_cols + jnp.arange(share_cols, dtype=jnp.int32)
    block_ids = col_group * col_blocks + jnp.arange(col_blocks, dtype=jnp.int32)
    kept, owner_width, within = block_mask(block_ids, column_ids, rowblocks, counts, widths)
    negated = jnp.where(
        kept[:, None, :], -summed.reshape(col_blocks, B, share_cols), jnp.zeros((), jnp.float32)
    )
    selected_inverse = negated.reshape(inverse_rows, share_cols).astype(jnp.bfloat16)
    groups = max(1, share_cols // B)
    left_side = across.reshape(inverse_rows, groups, width_cols // groups).astype(jnp.float32)
    right_side = summed.reshape(inverse_rows, groups, share_cols // groups)
    quadratic = jnp.einsum(
        "rnb,rnc->bnc", left_side, right_side, precision=lax.Precision.HIGHEST
    ).reshape(B, share_cols)
    quadratic = lax.psum(quadratic.astype(jnp.bfloat16), "pcol").astype(jnp.float32)
    corner = (jnp.arange(B, dtype=jnp.int32)[:, None] < owner_width[None, :]) & (
        within < owner_width
    )[None, :]
    diagonal_blocks = jnp.where(corner, dinv, jnp.zeros((), jnp.float32)) + quadratic
    return (selected_inverse, diagonal_blocks)


def level_kernel(
    n_z, n_x,
    a_ref, lp_ref, dinv_ref, rb_ref, cnt_ref, wid_ref,
    sel_ref, diag_ref,
    a_nb, fbuf, froot, psend, prec, pown, pbf, pnb, dpart, drec, dall,
    a_sem, fsend, frecv, rsend, rrecv, psend_sem, prec_sem, xsem_s, xsem_r,
    d1_s, d1_r, d2_s, d2_r,
):
    p = lax.axis_index("prow")
    c = lax.axis_index("pcol")
    z = lax.div(c, n_x)
    x = lax.rem(c, n_x)
    xo = 1 - x
    rows = a_ref.shape[0]
    H = 128
    halves = B // H
    slots = rb_ref.shape[1]
    row_blocks = lp_ref.shape[0] // B
    out_blocks = rows // B
    slice_rows = B // n_z

    def live(block, node):
        count = cnt_ref[node]
        hit = jnp.int32(0)
        for i in range(slots):
            hit += jnp.where((rb_ref[node, i] == block) & (i < count), 1, 0)
        return hit

    def remote(src, dst, s_sem, r_sem, prow, pcol):
        return pltpu.make_async_remote_copy(
            src_ref=src, dst_ref=dst, send_sem=s_sem, recv_sem=r_sem,
            device_id=(prow, pcol), device_id_type=MESH,
        )

    barrier = pltpu.get_barrier_semaphore()
    for d in range(1, n_z * n_x):
        pl.semaphore_signal(barrier, inc=1, device_id=(p, lax.rem(c + d, n_z * n_x)), device_id_type=MESH)
    for d in range(1, n_z):
        pl.semaphore_signal(barrier, inc=1, device_id=(lax.rem(p + d, n_z), c), device_id_type=MESH)

    width = wid_ref[c]
    for b in range(row_blocks):
        limit = jnp.where(live(p * row_blocks + b, c) > 0, width, 0)
        for h in range(halves):
            cols = lax.broadcasted_iota(jnp.int32, (B, H), 1) + h * H
            value = lp_ref[b * B:(b + 1) * B, h * H:(h + 1) * H].astype(jnp.float32)
            fbuf[z, h, b * B:(b + 1) * B, :] = jnp.where(cols < limit, value, 0.0).astype(jnp.bfloat16)

    pl.semaphore_wait(barrier, n_z * n_x - 1 + n_z - 1)

    a_copy = remote(a_ref, a_nb, a_sem.at[0], a_sem.at[1], p, z * n_x + xo)

    def f_copy(s, h, way):
        return remote(
            fbuf.at[s, h], fbuf.at[s, h], fsend.at[way, s, h], frecv.at[s, h],
            p, (z + (1 - 2 * way)) * n_x + x,
        )

    def root_copy(s, h):
        return remote(fbuf.at[s, h], froot.at[h], rsend.at[s, h], rrecv.at[h], s, c)

    def part_copy(s, r, h):
        return remote(
            psend.at[s, r, h], prec.at[p, r, h], psend_sem.at[s, r, h], prec_sem.at[p, r, h], s, c
        )

    def x_copy(h):
        return remote(pbf.at[1, h], pnb.at[h], xsem_s.at[h], xsem_r.at[h], p, z * n_x + xo)

    def partial(s, r, h, left):
        value = jnp.dot(left[...], fbuf[s, h], preferred_element_type=jnp.float32)

        @pl.when(s == p)
        def _():
            pown[r, h] = value

        @pl.when(s != p)
        def _():
            psend[s, r, h] = value.astype(jnp.bfloat16)
            part_copy(s, r, h).start()

    def item(i):
        t = lax.div(i, 2 * halves)
        h = lax.rem(lax.div(i, 2), halves)
        way = lax.rem(i, 2)
        s = z - t * (1 - 2 * way)
        valid = (s >= 0) & (s < n_z) & ((t > 0) | (way == 0))
        return t, h, way, s, valid

    def root_send(s, h):
        @pl.when(p == z)
        def _():
            @pl.when(s != z)
            def _():
                root_copy(s, h).start()

            @pl.when(s == z)
            def _():
                froot[h] = fbuf[s, h]

    for h in range(halves):
        @pl.when(z < n_z - 1)
        def _():
            f_copy(z, h, 0).start()

        @pl.when(z > 0)
        def _():
            f_copy(z, h, 1).start()

    a_copy.start()

    def first(i, carry):
        t, h, way, s, valid = item(i)

        @pl.when(valid)
        def _():
            @pl.when(t > 0)
            def _():
                f_copy(s, h, way).wait_recv()
                onward = z + (1 - 2 * way)

                @pl.when((onward >= 0) & (onward < n_z))
                def _():
                    f_copy(s, h, way).start()

            root_send(s, h)
            partial(s, 0, h, a_ref)

        return carry

    early = (n_z - 1) * 2 * halves
    lax.fori_loop(0, early, first, 0)
    a_copy.wait_recv()

    def second(i, carry):
        t, h, way, s, valid = item(i)

        @pl.when(valid)
        def _():
            partial(s, 1, h, a_nb)

        return carry

    lax.fori_loop(0, early, second, 0)

    def third(i, carry):
        t, h, way, s, valid = item(i)

        @pl.when(valid)
        def _():
            f_copy(s, h, way).wait_recv()
            root_send(s, h)
            partial(s, 0, h, a_ref)
            partial(s, 1, h, a_nb)

        return carry

    lax.fori_loop(early, early + 2 * halves, third, 0)

    def total(r, h):
        value = pown[r, h]
        for d in range(1, n_z):
            q = lax.rem(p + d, n_z)
            remote(
                psend.at[p, r, h], prec.at[q, r, h], psend_sem.at[p, r, h], prec_sem.at[q, r, h], p, c
            ).wait_recv()
            value = value + prec[q, r, h].astype(jnp.float32)
        return value

    signs = [
        [jnp.where(live(c * out_blocks + b, 2 * p + (x if w == 0 else xo)) > 0, -1.0, 0.0) for b in range(out_blocks)]
        for w in range(2)
    ]

    def write(value, w, h):
        node = x if w == 0 else xo
        lane = pl.multiple_of(node * B + h * H, H)
        for b in range(out_blocks):
            sel_ref[b * B:(b + 1) * B, pl.ds(lane, H)] = (value[b * B:(b + 1) * B] * signs[w][b]).astype(jnp.bfloat16)

    for h in range(halves):
        pbf[1, h] = total(1, h).astype(jnp.bfloat16)
        x_copy(h).start()
        value = total(0, h)
        pbf[0, h] = value.astype(jnp.bfloat16)
        write(value, 0, h)

    for h in range(halves):
        @pl.when(p != z)
        def _():
            root_copy(p, h).wait_recv()
    for h in range(halves):
        for g in range(halves):
            value = jnp.zeros((H, H), jnp.float32)
            for r in range(2):
                start = pl.multiple_of((x if r == 0 else xo) * rows, rows)
                value += lax.dot_general(
                    froot[g, pl.ds(start, rows), :], pbf[r, h], (((0,), (0,)), ((), ())),
                    preferred_element_type=jnp.float32,
                )
            dpart[g * H:(g + 1) * H, h * H:(h + 1) * H] = value.astype(jnp.bfloat16)

    def d1_copy(to, own):
        return remote(
            dpart.at[pl.ds(pl.multiple_of(to * slice_rows, slice_rows), slice_rows)], drec.at[own],
            d1_s.at[to], d1_r.at[own], p, to * n_x + x,
        )

    for d in range(1, n_z):
        d1_copy(lax.rem(z + d, n_z), z).start()
    value = dpart[pl.ds(pl.multiple_of(z * slice_rows, slice_rows), slice_rows)].astype(jnp.float32)
    for d in range(1, n_z):
        q = lax.rem(z + d, n_z)
        d1_copy(q, q).wait_recv()
        value = value + drec[q].astype(jnp.float32)
    dall[c] = value.astype(jnp.bfloat16)

    def d2_copy(to, own):
        return remote(dall.at[own], dall.at[own], d2_s.at[to], d2_r.at[own], p, to)

    for d in range(1, n_z * n_x):
        d2_copy(lax.rem(c + d, n_z * n_x), c).start()

    for h in range(halves):
        x_copy(h).wait_recv()
        write(pnb[h].astype(jnp.float32), 1, h)

    def corner(w, r):
        wide = wid_ref[2 * p + w]
        shape = (slice_rows, B)
        line = lax.broadcasted_iota(jnp.int32, shape, 0) + r * slice_rows
        col = lax.broadcasted_iota(jnp.int32, shape, 1)
        own = dinv_ref[r * slice_rows:(r + 1) * slice_rows, w * B:(w + 1) * B]
        return jnp.where((line < wide) & (col < wide), own, 0.0)

    for d in range(1, n_z * n_x):
        q = lax.rem(c + d, n_z * n_x)
        d2_copy(q, q).wait_recv()
    for r in range(n_z):
        for w in range(n_x):
            diag_ref[r * slice_rows:(r + 1) * slice_rows, w * B:(w + 1) * B] = (
                corner(w, r) + dall[r * n_x + w].astype(jnp.float32)
            )

    a_copy.wait_send()
    for h in range(halves):
        x_copy(h).wait_send()
    for s in range(n_z):
        for h in range(halves):
            @pl.when((s <= z) & (z < n_z - 1))
            def _():
                f_copy(s, h, 0).wait_send()

            @pl.when((s >= z) & (z > 0))
            def _():
                f_copy(s, h, 1).wait_send()

            @pl.when((p == z) & (s != z))
            def _():
                root_copy(s, h).wait_send()

            @pl.when(s != p)
            def _():
                for r in range(2):
                    part_copy(s, r, h).wait_send()
    for d in range(1, n_z):
        d1_copy(lax.rem(z + d, n_z), z).wait_send()
    for d in range(1, n_z * n_x):
        d2_copy(lax.rem(c + d, n_z * n_x), c).wait_send()


def fused(n_prow, n_pcol, ainv, lpanel, dinv, rowblocks, counts, widths):
    n_z, n_x = n_prow, 2
    rows, depth = ainv.shape
    bf, f32, H = jnp.bfloat16, jnp.float32, 128
    halves = B // H
    vmem = pl.BlockSpec(memory_space=pltpu.VMEM)
    smem = pl.BlockSpec(memory_space=pltpu.SMEM)
    dma = pltpu.SemaphoreType.DMA
    return pl.pallas_call(
        functools.partial(level_kernel, n_z, n_x),
        out_shape=(
            jax.ShapeDtypeStruct((rows, dinv.shape[1]), bf),
            jax.ShapeDtypeStruct(dinv.shape, f32),
        ),
        in_specs=[vmem] * 3 + [smem] * 3,
        out_specs=(vmem, vmem),
        scratch_shapes=[
            pltpu.VMEM((rows, depth), bf),
            pltpu.VMEM((n_z, halves, depth, H), bf),
            pltpu.VMEM((halves, depth, H), bf),
            pltpu.VMEM((n_z, 2, halves, rows, H), bf),
            pltpu.VMEM((n_z, 2, halves, rows, H), bf),
            pltpu.VMEM((2, halves, rows, H), f32),
            pltpu.VMEM((2, halves, rows, H), bf),
            pltpu.VMEM((halves, rows, H), bf),
            pltpu.VMEM((B, B), bf),
            pltpu.VMEM((n_z, B // n_z, B), bf),
            pltpu.VMEM((n_z * n_x, B // n_z, B), bf),
            dma((2,)),
            dma((2, n_z, halves)),
            dma((n_z, halves)),
            dma((n_z, halves)),
            dma((halves,)),
            dma((n_z, 2, halves)),
            dma((n_z, 2, halves)),
            dma((halves,)),
            dma((halves,)),
            dma((n_z,)),
            dma((n_z,)),
            dma((n_z * n_x,)),
            dma((n_z * n_x,)),
        ],
        compiler_params=pltpu.CompilerParams(
            collective_id=0, has_side_effects=True, vmem_limit_bytes=40 * 1024 * 1024
        ),
        cost_estimate=pl.CostEstimate(
            flops=2 * rows * depth * SNODES * B, bytes_accessed=4 * 1024 * 1024, transcendentals=0
        ),
    )(ainv, lpanel, dinv, rowblocks, counts, widths)


def solution(mesh):
    n_prow, n_pcol = mesh.shape["prow"], mesh.shape["pcol"]

    def step(ainv, lpanel, dinv, rowblocks, counts, widths):
        rows, depth = ainv.shape
        whole = n_pcol == 2 * n_prow and lpanel.shape[1] == B and dinv.shape[1] == 2 * B
        if whole and depth == 2 * rows and depth == lpanel.shape[0] and rows % B == 0 and B % (16 * n_prow) == 0:
            return fused(n_prow, n_pcol, ainv, lpanel, dinv, rowblocks, counts, widths)
        return per_device(ainv, lpanel, dinv, rowblocks, counts, widths)

    placed = (P("pcol", "prow"), P("prow", "pcol"), P(None, "prow"), P(), P(), P())
    return jax.shard_map(
        step,
        mesh=mesh,
        in_specs=placed,
        out_specs=(P("pcol", "prow"), P(None, "prow")),
        check_vma=False,
    )
```

```python
import functools

import jax
import jax.numpy as jnp
from jax import lax
from jax.experimental import pallas as pl
from jax.experimental.pallas import tpu as pltpu
from jax.sharding import PartitionSpec as P

MESH = pl.DeviceIdType.MESH

B = 256
SNODES = 8


def from_root(value, axis, source):
    kept = jnp.where(lax.axis_index(axis) == source, value, 0).astype(value.dtype)
    return lax.psum(kept, axis)


def block_mask(block_ids, column_ids, rowblocks, counts, widths):
    slot_total = rowblocks.shape[1]
    owner_node = column_ids // B
    within = column_ids % B
    chosen = owner_node[:, None] == jnp.arange(SNODES, dtype=jnp.int32)[None, :]
    owner_rows = jnp.sum(jnp.where(chosen[:, :, None], rowblocks[None, :, :], 0), axis=1)
    owner_count = jnp.sum(jnp.where(chosen, counts[None, :], 0), axis=1)
    owner_width = jnp.sum(jnp.where(chosen, widths[None, :], 0), axis=1)
    slot_live = jnp.arange(slot_total, dtype=jnp.int32)[None, :] < owner_count[:, None]
    matched = (owner_rows[None, :, :] == block_ids[:, None, None]) & slot_live[None, :, :]
    present = jnp.any(matched, axis=2) & (within < owner_width)[None, :]
    return (present, owner_width, within)


def per_device(ainv, lpanel, dinv, rowblocks, counts, widths):
    row_group = lax.axis_index("prow")
    col_group = lax.axis_index("pcol")
    panel_rows = lpanel.shape[0]
    panel_cols = lpanel.shape[1]
    inverse_rows = ainv.shape[0]
    share_cols = dinv.shape[1]
    row_blocks = panel_rows // B
    col_blocks = inverse_rows // B
    own_ids = row_group * row_blocks + jnp.arange(row_blocks, dtype=jnp.int32)
    own_cols = col_group * panel_cols + jnp.arange(panel_cols, dtype=jnp.int32)
    present, unused_width, unused_within = block_mask(own_ids, own_cols, rowblocks, counts, widths)
    masked = jnp.where(
        present[:, None, :], lpanel.reshape(row_blocks, B, panel_cols), jnp.zeros((), jnp.bfloat16)
    )
    masked = masked.reshape(panel_rows, panel_cols)
    gathered = lax.all_gather(masked, "pcol", axis=1, tiled=True)
    product = jnp.dot(ainv, gathered, preferred_element_type=jnp.float32)
    root_row = col_group * col_blocks // row_blocks
    offset = (col_group * col_blocks - root_row * row_blocks) * B
    own_rows = lax.dynamic_slice_in_dim(gathered, offset, inverse_rows, 0)
    width_cols = max(share_cols, B)
    first_col = row_group * share_cols // width_cols * width_cols
    summed = lax.psum_scatter(
        product.astype(jnp.bfloat16), "prow", scatter_dimension=1, tiled=True
    ).astype(jnp.float32)
    whole_rows = from_root(own_rows, "prow", root_row)
    across = lax.dynamic_slice_in_dim(whole_rows, first_col, width_cols, 1)
    column_ids = row_group * share_cols + jnp.arange(share_cols, dtype=jnp.int32)
    block_ids = col_group * col_blocks + jnp.arange(col_blocks, dtype=jnp.int32)
    kept, owner_width, within = block_mask(block_ids, column_ids, rowblocks, counts, widths)
    negated = jnp.where(
        kept[:, None, :], -summed.reshape(col_blocks, B, share_cols), jnp.zeros((), jnp.float32)
    )
    selected_inverse = negated.reshape(inverse_rows, share_cols).astype(jnp.bfloat16)
    groups = max(1, share_cols // B)
    left_side = across.reshape(inverse_rows, groups, width_cols // groups).astype(jnp.float32)
    right_side = summed.reshape(inverse_rows, groups, share_cols // groups)
    quadratic = jnp.einsum(
        "rnb,rnc->bnc", left_side, right_side, precision=lax.Precision.HIGHEST
    ).reshape(B, share_cols)
    quadratic = lax.psum(quadratic.astype(jnp.bfloat16), "pcol").astype(jnp.float32)
    corner = (jnp.arange(B, dtype=jnp.int32)[:, None] < owner_width[None, :]) & (
        within < owner_width
    )[None, :]
    diagonal_blocks = jnp.where(corner, dinv, jnp.zeros((), jnp.float32)) + quadratic
    return (selected_inverse, diagonal_blocks)


def level_kernel(
    n_z, n_x,
    a_hbm, lp_hbm, dinv_hbm, rb_hbm, cnt_hbm, wid_hbm,
    sel_ref, diag_ref,
    a_buf, lp_ref, dinv_ref, rb_ref, cnt_ref, wid_ref,
    fbuf, froot, froot_t, pown, pkeep, pair_out, pair_in, cross_out, cross_in, part_out, part_in,
    pall, pbf, pnb, dpart, drec, dall,
    in_sem, a_sem, fsend, frecv, rsend, rrecv,
    pair_s, pair_r, cross_s, cross_r, part_s, part_r, xsem_s, xsem_r,
    d1_s, d1_r, d2_s, d2_r,
):
    p = lax.axis_index("prow")
    c = lax.axis_index("pcol")
    z = lax.div(c, n_x)
    x = lax.rem(c, n_x)
    xo = 1 - x
    y = lax.div(p, 2)
    core = lax.rem(p, 2)
    mate = 2 * y + 1 - core
    rows = a_hbm.shape[0]
    H = 128
    halves = B // H
    slots = rb_ref.shape[1]
    row_blocks = lp_ref.shape[0] // B
    out_blocks = rows // B
    slice_rows = B // n_z

    fetches = [
        pltpu.make_async_copy(src, dst, in_sem.at[i])
        for i, (src, dst) in enumerate(
            [
                (rb_hbm, rb_ref), (cnt_hbm, cnt_ref), (wid_hbm, wid_ref),
                (lp_hbm, lp_ref), (a_hbm, a_buf.at[0]), (dinv_hbm, dinv_ref),
            ]
        )
    ]
    for fetch in fetches:
        fetch.start()

    def live(block, node):
        count = cnt_ref[node]
        hit = jnp.int32(0)
        for i in range(slots):
            hit += jnp.where((rb_ref[node, i] == block) & (i < count), 1, 0)
        return hit

    def remote(src, dst, s_sem, r_sem, prow, pcol):
        return pltpu.make_async_remote_copy(
            src_ref=src, dst_ref=dst, send_sem=s_sem, recv_sem=r_sem,
            device_id=(prow, pcol), device_id_type=MESH,
        )

    barrier = pltpu.get_barrier_semaphore()
    for d in range(1, n_z * n_x):
        pl.semaphore_signal(barrier, inc=1, device_id=(p, lax.rem(c + d, n_z * n_x)), device_id_type=MESH)
    for d in range(1, n_z):
        pl.semaphore_signal(barrier, inc=1, device_id=(lax.rem(p + d, n_z), c), device_id_type=MESH)

    a_copy = remote(a_hbm, a_buf.at[1], a_sem.at[0], a_sem.at[1], p, z * n_x + xo)

    def f_copy(s, h, way):
        return remote(
            fbuf.at[s, h], fbuf.at[s, h], fsend.at[way, s, h], frecv.at[s, h],
            p, (z + (1 - 2 * way)) * n_x + x,
        )

    def root_copy(s, h):
        return remote(fbuf.at[s, h], froot.at[h], rsend.at[s, h], rrecv.at[h], s, c)

    def part_copy(r, h):
        return remote(part_out.at[r, h], part_in.at[r, h], part_s.at[r, h], part_r.at[r, h], mate, c)

    def pair_copy(e, h):
        return remote(pair_out.at[e, h], pair_in.at[e, h], pair_s.at[e, h], pair_r.at[e, h], mate, c)

    def cross_copy(e, r, h):
        return remote(
            cross_out.at[e, h], cross_in.at[r, h], cross_s.at[e, h], cross_r.at[r, h], 2 * (1 - y) + e, c
        )

    def x_copy(h):
        return remote(pbf.at[h], pnb.at[h], xsem_s.at[h], xsem_r.at[h], p, z * n_x + xo)

    def partial(s, r, h):
        value = jnp.dot(a_buf[r], fbuf[s, h], preferred_element_type=jnp.float32)
        e = lax.rem(s, 2)
        same = lax.div(s, 2) == y

        @pl.when(same & (s == p))
        def _():
            pown[r, h] = value

        @pl.when(same & (s != p))
        def _():
            part_out[r, h] = value.astype(jnp.bfloat16)
            part_copy(r, h).start()

        @pl.when(jnp.logical_not(same) & (r == core))
        def _():
            pkeep[e, h] = value

        @pl.when(jnp.logical_not(same) & (r != core))
        def _():
            pair_out[e, h] = value.astype(jnp.bfloat16)
            pair_copy(e, h).start()

    def finalize(s, r, h):
        e = lax.rem(s, 2)

        @pl.when((lax.div(s, 2) != y) & (r == core))
        def _():
            pair_copy(e, h).wait_recv()
            cross_out[e, h] = (pkeep[e, h] + pair_in[e, h].astype(jnp.float32)).astype(jnp.bfloat16)
            cross_copy(e, r, h).start()

    def root_send(s, h):
        @pl.when(p == z)
        def _():
            @pl.when(s != z)
            def _():
                root_copy(s, h).start()

            @pl.when(s == z)
            def _():
                froot[h] = fbuf[s, h]

    for fetch in fetches[:4]:
        fetch.wait()
    width = wid_ref[c]
    limits = [jnp.where(live(p * row_blocks + b, c) > 0, width, 0) for b in range(row_blocks)]
    for h in range(halves):
        for b in range(row_blocks):
            cols = lax.broadcasted_iota(jnp.int32, (B, H), 1) + h * H
            value = lp_ref[b * B:(b + 1) * B, h * H:(h + 1) * H].astype(jnp.float32)
            fbuf[z, h, b * B:(b + 1) * B, :] = jnp.where(cols < limits[b], value, 0.0).astype(jnp.bfloat16)
        if h == 0:
            pl.semaphore_wait(barrier, n_z * n_x - 1 + n_z - 1)
            a_copy.start()

        @pl.when(z < n_z - 1)
        def _():
            f_copy(z, h, 0).start()

        @pl.when(z > 0)
        def _():
            f_copy(z, h, 1).start()
    for fetch in fetches[4:]:
        fetch.wait()

    def both(j, act):
        t = lax.div(j, halves)
        h = lax.rem(j, halves)
        for way in range(2):
            s = z - t * (1 - 2 * way)
            valid = (s >= 0) & (s < n_z)
            if way == 1:
                valid = valid & (t > 0)

            @pl.when(valid)
            def _():
                act(t, h, way, s)

    def arrive(t, h, way, s):
        @pl.when(t > 0)
        def _():
            f_copy(s, h, way).wait_recv()
            onward = z + (1 - 2 * way)

            @pl.when((onward >= 0) & (onward < n_z))
            def _():
                f_copy(s, h, way).start()

        root_send(s, h)

    def first_act(t, h, way, s):
        arrive(t, h, way, s)
        partial(s, 0, h)

    def first(j, carry):
        both(j, first_act)
        both(j, lambda t, h, way, s: finalize(s, 0, h))
        return carry

    early = (n_z - 1) * halves
    lax.fori_loop(0, early, first, 0)
    a_copy.wait_recv()

    def second(j, carry):
        @pl.when(j < early)
        def _():
            both(j, lambda t, h, way, s: partial(s, 1, h))

        @pl.when(j > 0)
        def _():
            both(j - 1, lambda t, h, way, s: finalize(s, 1, h))

        return carry

    lax.fori_loop(0, early + 1, second, 0)

    def third_act(t, h, way, s):
        arrive(t, h, way, s)

        def each(i, carry):
            partial(s, jnp.where(i == 0, 1 - core, core), h)
            return carry

        lax.fori_loop(0, 2, each, 0)
        finalize(s, core, h)

    def third(j, carry):
        both(j, third_act)
        return carry

    lax.fori_loop(early, early + halves, third, 0)

    def total(r, h):
        part_copy(r, h).wait_recv()
        cross_copy(core, r, h).wait_recv()
        return pown[r, h] + part_in[r, h].astype(jnp.float32) + cross_in[r, h].astype(jnp.float32)

    signs = [
        [jnp.where(live(c * out_blocks + b, 2 * p + (x if w == 0 else xo)) > 0, -1.0, 0.0) for b in range(out_blocks)]
        for w in range(2)
    ]

    def write(value, w, h):
        node = x if w == 0 else xo
        lane = pl.multiple_of(node * B + h * H, H)
        for b in range(out_blocks):
            sel_ref[b * B:(b + 1) * B, pl.ds(lane, H)] = (value[b * B:(b + 1) * B] * signs[w][b]).astype(jnp.bfloat16)

    for h in range(halves):
        @pl.when(p != z)
        def _():
            root_copy(p, h).wait_recv()
        froot_t[h * H:(h + 1) * H, :] = jnp.transpose(froot[h])
        value = total(1, h).astype(jnp.bfloat16)
        pbf[h] = value
        x_copy(h).start()
        pall[pl.ds(pl.multiple_of(xo * rows, rows), rows), h * H:(h + 1) * H] = value
        value = total(0, h)
        pall[pl.ds(pl.multiple_of(x * rows, rows), rows), h * H:(h + 1) * H] = value.astype(jnp.bfloat16)
        if h < halves - 1:
            write(value, 0, h)

    dpart[...] = jnp.dot(froot_t[...], pall[...], preferred_element_type=jnp.float32).astype(jnp.bfloat16)

    def d1_copy(to, own):
        return remote(
            dpart.at[pl.ds(pl.multiple_of(to * slice_rows, slice_rows), slice_rows)], drec.at[own],
            d1_s.at[to], d1_r.at[own], p, to * n_x + x,
        )

    for d in range(1, n_z):
        d1_copy(lax.rem(z + d, n_z), z).start()
    write(value, 0, halves - 1)
    value = dpart[pl.ds(pl.multiple_of(z * slice_rows, slice_rows), slice_rows)].astype(jnp.float32)
    for d in range(1, n_z):
        q = lax.rem(z + d, n_z)
        d1_copy(q, q).wait_recv()
        value = value + drec[q].astype(jnp.float32)
    dall[c] = value.astype(jnp.bfloat16)

    def d2_copy(to, own):
        return remote(dall.at[own], dall.at[own], d2_s.at[to], d2_r.at[own], p, to)

    for d in range(1, n_z * n_x):
        d2_copy(lax.rem(c + d, n_z * n_x), c).start()

    for h in range(halves):
        x_copy(h).wait_recv()
        write(pnb[h].astype(jnp.float32), 1, h)

    def corner(w, r):
        wide = wid_ref[2 * p + w]
        shape = (slice_rows, B)
        line = lax.broadcasted_iota(jnp.int32, shape, 0) + r * slice_rows
        col = lax.broadcasted_iota(jnp.int32, shape, 1)
        own = dinv_ref[r * slice_rows:(r + 1) * slice_rows, w * B:(w + 1) * B]
        return jnp.where((line < wide) & (col < wide), own, 0.0)

    for d in range(1, n_z * n_x):
        q = lax.rem(c + d, n_z * n_x)
        d2_copy(q, q).wait_recv()
    for r in range(n_z):
        for w in range(n_x):
            diag_ref[r * slice_rows:(r + 1) * slice_rows, w * B:(w + 1) * B] = (
                corner(w, r) + dall[r * n_x + w].astype(jnp.float32)
            )

    a_copy.wait_send()
    for h in range(halves):
        x_copy(h).wait_send()
        for r in range(2):
            part_copy(r, h).wait_send()
        for e in range(2):
            pair_copy(e, h).wait_send()
            cross_copy(e, core, h).wait_send()
    for s in range(n_z):
        for h in range(halves):
            @pl.when((s <= z) & (z < n_z - 1))
            def _():
                f_copy(s, h, 0).wait_send()

            @pl.when((s >= z) & (z > 0))
            def _():
                f_copy(s, h, 1).wait_send()

            @pl.when((p == z) & (s != z))
            def _():
                root_copy(s, h).wait_send()
    for d in range(1, n_z):
        d1_copy(lax.rem(z + d, n_z), z).wait_send()
    for d in range(1, n_z * n_x):
        d2_copy(lax.rem(c + d, n_z * n_x), c).wait_send()


def fused(n_prow, n_pcol, ainv, lpanel, dinv, rowblocks, counts, widths):
    n_z, n_x = n_prow, 2
    rows, depth = ainv.shape
    bf, f32, H = jnp.bfloat16, jnp.float32, 128
    halves = B // H
    vmem = pl.BlockSpec(memory_space=pltpu.VMEM)
    hbm = pl.BlockSpec(memory_space=pltpu.HBM)
    dma = pltpu.SemaphoreType.DMA
    piece = (2, halves, rows, H)
    return pl.pallas_call(
        functools.partial(level_kernel, n_z, n_x),
        out_shape=(
            jax.ShapeDtypeStruct((rows, dinv.shape[1]), bf),
            jax.ShapeDtypeStruct(dinv.shape, f32),
        ),
        in_specs=[hbm] * 6,
        out_specs=(vmem, vmem),
        scratch_shapes=[
            pltpu.VMEM((2, rows, depth), bf),
            pltpu.VMEM(lpanel.shape, bf),
            pltpu.VMEM(dinv.shape, f32),
            pltpu.SMEM(rowblocks.shape, jnp.int32),
            pltpu.SMEM(counts.shape, jnp.int32),
            pltpu.SMEM(widths.shape, jnp.int32),
            pltpu.VMEM((n_z, halves, depth, H), bf),
            pltpu.VMEM((halves, depth, H), bf),
            pltpu.VMEM((B, depth), bf),
            pltpu.VMEM(piece, f32),
            pltpu.VMEM(piece, f32),
        ]
        + [pltpu.VMEM(piece, bf)] * 6
        + [
            pltpu.VMEM((depth, B), bf),
            pltpu.VMEM((halves, rows, H), bf),
            pltpu.VMEM((halves, rows, H), bf),
            pltpu.VMEM((B, B), bf),
            pltpu.VMEM((n_z, B // n_z, B), bf),
            pltpu.VMEM((n_z * n_x, B // n_z, B), bf),
            dma((6,)),
            dma((2,)),
            dma((2, n_z, halves)),
            dma((n_z, halves)),
            dma((n_z, halves)),
            dma((halves,)),
        ]
        + [dma((2, halves))] * 6
        + [
            dma((halves,)),
            dma((halves,)),
            dma((n_z,)),
            dma((n_z,)),
            dma((n_z * n_x,)),
            dma((n_z * n_x,)),
        ],
        compiler_params=pltpu.CompilerParams(
            collective_id=0, has_side_effects=True, vmem_limit_bytes=60 * 1024 * 1024
        ),
        cost_estimate=pl.CostEstimate(
            flops=2 * rows * depth * SNODES * B, bytes_accessed=4 * 1024 * 1024, transcendentals=0
        ),
    )(ainv, lpanel, dinv, rowblocks, counts, widths)


def solution(mesh):
    n_prow, n_pcol = mesh.shape["prow"], mesh.shape["pcol"]

    def step(ainv, lpanel, dinv, rowblocks, counts, widths):
        rows, depth = ainv.shape
        whole = n_prow == 4 and n_pcol == 8 and lpanel.shape[1] == B and dinv.shape[1] == 2 * B
        if whole and depth == 2 * rows and depth == lpanel.shape[0] and rows % B == 0 and B % (16 * n_prow) == 0:
            return fused(n_prow, n_pcol, ainv, lpanel, dinv, rowblocks, counts, widths)
        return per_device(ainv, lpanel, dinv, rowblocks, counts, widths)

    placed = (P("pcol", "prow"), P("prow", "pcol"), P(None, "prow"), P(), P(), P())
    return jax.shard_map(
        step,
        mesh=mesh,
        in_specs=placed,
        out_specs=(P("pcol", "prow"), P(None, "prow")),
        check_vma=False,
    )
```

```python
import functools

import jax
import jax.numpy as jnp
from jax import lax
from jax.experimental import pallas as pl
from jax.experimental.pallas import tpu as pltpu
from jax.sharding import PartitionSpec as P

MESH = pl.DeviceIdType.MESH

B = 256
SNODES = 8


def from_root(value, axis, source):
    kept = jnp.where(lax.axis_index(axis) == source, value, 0).astype(value.dtype)
    return lax.psum(kept, axis)


def block_mask(block_ids, column_ids, rowblocks, counts, widths):
    slot_total = rowblocks.shape[1]
    owner_node = column_ids // B
    within = column_ids % B
    chosen = owner_node[:, None] == jnp.arange(SNODES, dtype=jnp.int32)[None, :]
    owner_rows = jnp.sum(jnp.where(chosen[:, :, None], rowblocks[None, :, :], 0), axis=1)
    owner_count = jnp.sum(jnp.where(chosen, counts[None, :], 0), axis=1)
    owner_width = jnp.sum(jnp.where(chosen, widths[None, :], 0), axis=1)
    slot_live = jnp.arange(slot_total, dtype=jnp.int32)[None, :] < owner_count[:, None]
    matched = (owner_rows[None, :, :] == block_ids[:, None, None]) & slot_live[None, :, :]
    present = jnp.any(matched, axis=2) & (within < owner_width)[None, :]
    return (present, owner_width, within)


def per_device(ainv, lpanel, dinv, rowblocks, counts, widths):
    row_group = lax.axis_index("prow")
    col_group = lax.axis_index("pcol")
    panel_rows = lpanel.shape[0]
    panel_cols = lpanel.shape[1]
    inverse_rows = ainv.shape[0]
    share_cols = dinv.shape[1]
    row_blocks = panel_rows // B
    col_blocks = inverse_rows // B
    own_ids = row_group * row_blocks + jnp.arange(row_blocks, dtype=jnp.int32)
    own_cols = col_group * panel_cols + jnp.arange(panel_cols, dtype=jnp.int32)
    present, unused_width, unused_within = block_mask(own_ids, own_cols, rowblocks, counts, widths)
    masked = jnp.where(
        present[:, None, :], lpanel.reshape(row_blocks, B, panel_cols), jnp.zeros((), jnp.bfloat16)
    )
    masked = masked.reshape(panel_rows, panel_cols)
    gathered = lax.all_gather(masked, "pcol", axis=1, tiled=True)
    product = jnp.dot(ainv, gathered, preferred_element_type=jnp.float32)
    root_row = col_group * col_blocks // row_blocks
    offset = (col_group * col_blocks - root_row * row_blocks) * B
    own_rows = lax.dynamic_slice_in_dim(gathered, offset, inverse_rows, 0)
    width_cols = max(share_cols, B)
    first_col = row_group * share_cols // width_cols * width_cols
    summed = lax.psum_scatter(
        product.astype(jnp.bfloat16), "prow", scatter_dimension=1, tiled=True
    ).astype(jnp.float32)
    whole_rows = from_root(own_rows, "prow", root_row)
    across = lax.dynamic_slice_in_dim(whole_rows, first_col, width_cols, 1)
    column_ids = row_group * share_cols + jnp.arange(share_cols, dtype=jnp.int32)
    block_ids = col_group * col_blocks + jnp.arange(col_blocks, dtype=jnp.int32)
    kept, owner_width, within = block_mask(block_ids, column_ids, rowblocks, counts, widths)
    negated = jnp.where(
        kept[:, None, :], -summed.reshape(col_blocks, B, share_cols), jnp.zeros((), jnp.float32)
    )
    selected_inverse = negated.reshape(inverse_rows, share_cols).astype(jnp.bfloat16)
    groups = max(1, share_cols // B)
    left_side = across.reshape(inverse_rows, groups, width_cols // groups).astype(jnp.float32)
    right_side = summed.reshape(inverse_rows, groups, share_cols // groups)
    quadratic = jnp.einsum(
        "rnb,rnc->bnc", left_side, right_side, precision=lax.Precision.HIGHEST
    ).reshape(B, share_cols)
    quadratic = lax.psum(quadratic.astype(jnp.bfloat16), "pcol").astype(jnp.float32)
    corner = (jnp.arange(B, dtype=jnp.int32)[:, None] < owner_width[None, :]) & (
        within < owner_width
    )[None, :]
    diagonal_blocks = jnp.where(corner, dinv, jnp.zeros((), jnp.float32)) + quadratic
    return (selected_inverse, diagonal_blocks)


PIECES = 4


def handoff_kernel(sel_in, diag_in, sel_out, diag_out, sem):
    copies = []
    for k, (src, dst) in enumerate([(sel_in, sel_out), (diag_in, diag_out)]):
        part = src.shape[0] // PIECES
        for i in range(PIECES):
            piece = pl.ds(i * part, part)
            copies.append(pltpu.make_async_copy(src.at[piece], dst.at[piece], sem.at[k * PIECES + i]))
    for copy in copies:
        copy.start()
    for copy in copies:
        copy.wait()


def level_kernel(
    n_z, n_x,
    a_hbm, lp_hbm, dinv_hbm, rb_hbm, cnt_hbm, wid_hbm,
    sel_ref, diag_ref,
    a_buf, lp_ref, dinv_ref, rb_ref, cnt_ref, wid_ref,
    fbuf, f_t, pkeep, pair_out, pair_in, csum, cin, pall, pbf, pnb, dpart, drec, dall,
    in_sem, a_sem, fsend, frecv, pair_s, pair_r, own_s, root_s, cin_r, xsem_s, xsem_r,
    d1_s, d1_r, d2_s, d2_r,
):
    p = lax.axis_index("prow")
    c = lax.axis_index("pcol")
    z = lax.div(c, n_x)
    x = lax.rem(c, n_x)
    xo = 1 - x
    y = lax.div(p, 2)
    core = lax.rem(p, 2)
    mate = 2 * y + 1 - core
    rows = a_hbm.shape[0]
    H = 128
    halves = B // H
    slots = rb_ref.shape[1]
    row_blocks = lp_ref.shape[0] // B
    out_blocks = rows // B
    slice_rows = B // n_z

    fetches = [
        pltpu.make_async_copy(src, dst, in_sem.at[i])
        for i, (src, dst) in enumerate(
            [
                (rb_hbm, rb_ref), (cnt_hbm, cnt_ref), (wid_hbm, wid_ref),
                (lp_hbm, lp_ref), (a_hbm, a_buf.at[0]), (dinv_hbm, dinv_ref),
            ]
        )
    ]
    for fetch in fetches:
        fetch.start()

    def live(block, node):
        count = cnt_ref[node]
        hit = jnp.int32(0)
        for i in range(slots):
            hit += jnp.where((rb_ref[node, i] == block) & (i < count), 1, 0)
        return hit

    def remote(src, dst, s_sem, r_sem, prow, pcol):
        return pltpu.make_async_remote_copy(
            src_ref=src, dst_ref=dst, send_sem=s_sem, recv_sem=r_sem,
            device_id=(prow, pcol), device_id_type=MESH,
        )

    barrier = pltpu.get_barrier_semaphore()
    spot = z * n_z + p
    for d in range(1, n_z * n_z):
        q = lax.rem(spot + d, n_z * n_z)
        pl.semaphore_signal(
            barrier, inc=1, device_id=(lax.rem(q, n_z), lax.div(q, n_z) * n_x + x), device_id_type=MESH
        )
    for d in range(n_z):
        pl.semaphore_signal(barrier, inc=1, device_id=(p, d * n_x + xo), device_id_type=MESH)

    a_copy = remote(a_hbm, a_buf.at[1], a_sem.at[0], a_sem.at[1], p, z * n_x + xo)

    def f_copy(s, h, way):
        return remote(
            fbuf.at[s, h], fbuf.at[s, h], fsend.at[way, s, h], frecv.at[s, h],
            p, (z + (1 - 2 * way)) * n_x + x,
        )

    def pair_copy(s, h):
        return remote(pair_out.at[s, h], pair_in.at[s, h], pair_s.at[s, h], pair_r.at[s, h], mate, c)

    def sum_copy(s, h, sem, to):
        return remote(csum.at[s, h], cin.at[s, y, core, h], sem.at[s, h], cin_r.at[s, y, core, h], to, c)

    def x_copy(h):
        return remote(pbf.at[h], pnb.at[h], xsem_s.at[h], xsem_r.at[h], p, z * n_x + xo)

    def partial(s, r, h):
        value = jnp.dot(a_buf[r], fbuf[s, h], preferred_element_type=jnp.float32)

        @pl.when(r == core)
        def _():
            pkeep[s, h] = value

        @pl.when(r != core)
        def _():
            pair_out[s, h] = value.astype(jnp.bfloat16)
            pair_copy(s, h).start()

    def finalize(s, r, h):
        @pl.when(r == core)
        def _():
            pair_copy(s, h).wait_recv()
            value = (pkeep[s, h] + pair_in[s, h].astype(jnp.float32)).astype(jnp.bfloat16)
            csum[s, h] = value

            @pl.when((s == p) | (z == p))
            def _():
                cin[s, y, core, h] = value

            @pl.when((s != z) & (z != p))
            def _():
                sum_copy(s, h, root_s, z).start()

            @pl.when(s != p)
            def _():
                sum_copy(s, h, own_s, s).start()

    for fetch in fetches[:4]:
        fetch.wait()
    width = wid_ref[c]
    limits = [jnp.where(live(p * row_blocks + b, c) > 0, width, 0) for b in range(row_blocks)]
    for h in range(halves):
        for b in range(row_blocks):
            cols = lax.broadcasted_iota(jnp.int32, (B, H), 1) + h * H
            value = lp_ref[b * B:(b + 1) * B, h * H:(h + 1) * H].astype(jnp.float32)
            fbuf[z, h, b * B:(b + 1) * B, :] = jnp.where(cols < limits[b], value, 0.0).astype(jnp.bfloat16)
        if h == 0:
            pl.semaphore_wait(barrier, n_z * n_z - 1 + n_z)
            a_copy.start()

        @pl.when(z < n_z - 1)
        def _():
            f_copy(z, h, 0).start()

        @pl.when(z > 0)
        def _():
            f_copy(z, h, 1).start()
    for fetch in fetches[4:]:
        fetch.wait()

    def both(j, act):
        t = lax.div(j, halves)
        h = lax.rem(j, halves)
        for way in range(2):
            s = z - t * (1 - 2 * way)
            valid = (s >= 0) & (s < n_z)
            if way == 1:
                valid = valid & (t > 0)

            @pl.when(valid)
            def _():
                act(t, h, way, s)

    def arrive(t, h, way, s):
        @pl.when(t > 0)
        def _():
            f_copy(s, h, way).wait_recv()
            onward = z + (1 - 2 * way)

            @pl.when((onward >= 0) & (onward < n_z))
            def _():
                f_copy(s, h, way).start()

    def first_act(t, h, way, s):
        arrive(t, h, way, s)
        partial(s, 0, h)

    def first(j, carry):
        both(j, first_act)
        both(j, lambda t, h, way, s: finalize(s, 0, h))
        return carry

    early = (n_z - 1) * halves
    lax.fori_loop(0, early, first, 0)
    a_copy.wait_recv()

    def second(j, carry):
        @pl.when(j < early)
        def _():
            both(j, lambda t, h, way, s: partial(s, 1, h))

        @pl.when(j > 0)
        def _():
            both(j - 1, lambda t, h, way, s: finalize(s, 1, h))

        return carry

    lax.fori_loop(0, early + 1, second, 0)

    def third_act(t, h, way, s):
        arrive(t, h, way, s)

        def each(i, carry):
            partial(s, jnp.where(i == 0, 1 - core, core), h)
            return carry

        lax.fori_loop(0, 2, each, 0)
        finalize(s, core, h)

    def third(j, carry):
        both(j, third_act)
        return carry

    def total(s, r, h, wait):
        for g in range(2):
            @pl.when(wait & (2 * g + r != p))
            def _():
                remote(
                    csum.at[s, h], cin.at[s, g, r, h], own_s.at[s, h], cin_r.at[s, g, r, h], p, c
                ).wait_recv()
        return cin[s, 0, r, h].astype(jnp.float32) + cin[s, 1, r, h].astype(jnp.float32)

    def d1_copy(s, to, own):
        return remote(
            dpart.at[s, pl.ds(pl.multiple_of(to * slice_rows, slice_rows), slice_rows)], drec.at[own],
            d1_s.at[s, to], d1_r.at[own], s, to * n_x + x,
        )

    def diag(s):
        for h in range(halves):
            f_t[h * H:(h + 1) * H, :] = jnp.transpose(fbuf[s, h])
        for h in range(halves):
            for r in range(2):
                start = pl.multiple_of((x if r == 0 else xo) * rows, rows)
                pall[pl.ds(start, rows), h * H:(h + 1) * H] = total(s, r, h, p == z).astype(jnp.bfloat16)
        dpart[s] = jnp.dot(f_t[...], pall[...], preferred_element_type=jnp.float32).astype(jnp.bfloat16)
        for to in range(n_z):
            @pl.when((s == z) & (z == to))
            def _():
                drec[z] = dpart[s, to * slice_rows:(to + 1) * slice_rows]

            @pl.when((s != z) | (z != to))
            def _():
                d1_copy(s, to, z).start()

    signs = [
        [jnp.where(live(c * out_blocks + b, 2 * p + (x if w == 0 else xo)) > 0, -1.0, 0.0) for b in range(out_blocks)]
        for w in range(2)
    ]

    def write(value, w, h):
        node = x if w == 0 else xo
        lane = pl.multiple_of(node * B + h * H, H)
        for b in range(out_blocks):
            sel_ref[b * B:(b + 1) * B, pl.ds(lane, H)] = (value[b * B:(b + 1) * B] * signs[w][b]).astype(jnp.bfloat16)

    def owner():
        for h in range(halves):
            pbf[h] = total(p, 1, h, p != z).astype(jnp.bfloat16)
            x_copy(h).start()
            write(total(p, 0, h, p != z), 0, h)

    @pl.when(p == z)
    def _():
        def early_diag(i, carry):
            t = lax.div(i, 2)
            way = lax.rem(i, 2)
            s = z - t * (1 - 2 * way)

            @pl.when((s >= 0) & (s < n_z) & ((t > 0) | (way == 0)))
            def _():
                diag(s)

            return carry

        lax.fori_loop(0, 2 * (n_z - 1), early_diag, 0)

    last = ((z == 0) & (p == n_z - 1)) | ((z == n_z - 1) & (p == 0))

    @pl.when(jnp.logical_not(last))
    def _():
        owner()

    lax.fori_loop(early, early + halves, third, 0)

    @pl.when((p == z) & ((z == 0) | (z == n_z - 1)))
    def _():
        diag(n_z - 1 - z)

    @pl.when(last)
    def _():
        owner()

    value = jnp.zeros((slice_rows, B), jnp.float32)
    for q in range(n_z):
        @pl.when((q != z) | (p != z))
        def _():
            d1_copy(q, z, q).wait_recv()
        value = value + drec[q].astype(jnp.float32)
    dall[c] = value.astype(jnp.bfloat16)

    def d2_copy(to, own):
        return remote(dall.at[own], dall.at[own], d2_s.at[to], d2_r.at[own], p, to)

    for d in range(1, n_z * n_x):
        d2_copy(lax.rem(c + d, n_z * n_x), c).start()

    for h in range(halves):
        x_copy(h).wait_recv()
        write(pnb[h].astype(jnp.float32), 1, h)

    def corner(w, r):
        wide = wid_ref[2 * p + w]
        shape = (slice_rows, B)
        line = lax.broadcasted_iota(jnp.int32, shape, 0) + r * slice_rows
        col = lax.broadcasted_iota(jnp.int32, shape, 1)
        own = dinv_ref[r * slice_rows:(r + 1) * slice_rows, w * B:(w + 1) * B]
        return jnp.where((line < wide) & (col < wide), own, 0.0)

    for d in range(1, n_z * n_x):
        q = lax.rem(c + d, n_z * n_x)
        d2_copy(q, q).wait_recv()
    for r in range(n_z):
        for w in range(n_x):
            diag_ref[r * slice_rows:(r + 1) * slice_rows, w * B:(w + 1) * B] = (
                corner(w, r) + dall[r * n_x + w].astype(jnp.float32)
            )

    a_copy.wait_send()
    for h in range(halves):
        x_copy(h).wait_send()
    for s in range(n_z):
        for h in range(halves):
            pair_copy(s, h).wait_send()

            @pl.when((s <= z) & (z < n_z - 1))
            def _():
                f_copy(s, h, 0).wait_send()

            @pl.when((s >= z) & (z > 0))
            def _():
                f_copy(s, h, 1).wait_send()

            @pl.when((s != z) & (z != p))
            def _():
                sum_copy(s, h, root_s, z).wait_send()

            @pl.when(s != p)
            def _():
                sum_copy(s, h, own_s, s).wait_send()
        for to in range(n_z):
            @pl.when((p == z) & ((s != z) | (z != to)))
            def _():
                d1_copy(s, to, z).wait_send()
    for d in range(1, n_z * n_x):
        d2_copy(lax.rem(c + d, n_z * n_x), c).wait_send()


def fused(n_prow, n_pcol, ainv, lpanel, dinv, rowblocks, counts, widths):
    n_z, n_x = n_prow, 2
    rows, depth = ainv.shape
    bf, f32, H = jnp.bfloat16, jnp.float32, 128
    halves = B // H
    vmem = pl.BlockSpec(memory_space=pltpu.VMEM)
    hbm = pl.BlockSpec(memory_space=pltpu.HBM)
    dma = pltpu.SemaphoreType.DMA
    piece = (n_z, halves, rows, H)
    results = pl.pallas_call(
        functools.partial(level_kernel, n_z, n_x),
        out_shape=(
            jax.ShapeDtypeStruct((rows, dinv.shape[1]), bf),
            jax.ShapeDtypeStruct(dinv.shape, f32),
        ),
        in_specs=[hbm] * 6,
        out_specs=(vmem, vmem),
        scratch_shapes=[
            pltpu.VMEM((2, rows, depth), bf),
            pltpu.VMEM(lpanel.shape, bf),
            pltpu.VMEM(dinv.shape, f32),
            pltpu.SMEM(rowblocks.shape, jnp.int32),
            pltpu.SMEM(counts.shape, jnp.int32),
            pltpu.SMEM(widths.shape, jnp.int32),
            pltpu.VMEM((n_z, halves, depth, H), bf),
            pltpu.VMEM((B, depth), bf),
            pltpu.VMEM(piece, f32),
            pltpu.VMEM(piece, bf),
            pltpu.VMEM(piece, bf),
            pltpu.VMEM(piece, bf),
            pltpu.VMEM((n_z, 2, 2, halves, rows, H), bf),
            pltpu.VMEM((depth, B), bf),
            pltpu.VMEM((halves, rows, H), bf),
            pltpu.VMEM((halves, rows, H), bf),
            pltpu.VMEM((n_z, B, B), bf),
            pltpu.VMEM((n_z, B // n_z, B), bf),
            pltpu.VMEM((n_z * n_x, B // n_z, B), bf),
            dma((6,)),
            dma((2,)),
            dma((2, n_z, halves)),
            dma((n_z, halves)),
        ]
        + [dma((n_z, halves))] * 4
        + [
            dma((n_z, 2, 2, halves)),
            dma((halves,)),
            dma((halves,)),
            dma((n_z, n_z)),
            dma((n_z,)),
            dma((n_z * n_x,)),
            dma((n_z * n_x,)),
        ],
        compiler_params=pltpu.CompilerParams(
            collective_id=0, has_side_effects=True, vmem_limit_bytes=60 * 1024 * 1024
        ),
        cost_estimate=pl.CostEstimate(
            flops=2 * rows * depth * SNODES * B, bytes_accessed=4 * 1024 * 1024, transcendentals=0
        ),
    )(ainv, lpanel, dinv, rowblocks, counts, widths)
    anywhere = pl.BlockSpec(memory_space=pl.ANY)
    return pl.pallas_call(
        handoff_kernel,
        out_shape=tuple(jax.ShapeDtypeStruct(r.shape, r.dtype) for r in results),
        in_specs=[anywhere] * 2,
        out_specs=(anywhere, anywhere),
        scratch_shapes=[dma((2 * PIECES,))],
        compiler_params=pltpu.CompilerParams(vmem_limit_bytes=60 * 1024 * 1024),
    )(*results)


def solution(mesh):
    n_prow, n_pcol = mesh.shape["prow"], mesh.shape["pcol"]

    def step(ainv, lpanel, dinv, rowblocks, counts, widths):
        rows, depth = ainv.shape
        whole = n_prow == 4 and n_pcol == 8 and lpanel.shape[1] == B and dinv.shape[1] == 2 * B
        if whole and depth == 2 * rows and depth == lpanel.shape[0] and rows % B == 0 and B % (16 * n_prow) == 0:
            return fused(n_prow, n_pcol, ainv, lpanel, dinv, rowblocks, counts, widths)
        return per_device(ainv, lpanel, dinv, rowblocks, counts, widths)

    placed = (P("pcol", "prow"), P("prow", "pcol"), P(None, "prow"), P(), P(), P())
    return jax.shard_map(
        step,
        mesh=mesh,
        in_specs=placed,
        out_specs=(P("pcol", "prow"), P(None, "prow")),
        check_vma=False,
    )
```

```python
import functools

import jax
import jax.numpy as jnp
from jax import lax
from jax.experimental import pallas as pl
from jax.experimental.pallas import tpu as pltpu
from jax.sharding import PartitionSpec as P

MESH = pl.DeviceIdType.MESH

B = 256
SNODES = 8


def from_root(value, axis, source):
    kept = jnp.where(lax.axis_index(axis) == source, value, 0).astype(value.dtype)
    return lax.psum(kept, axis)


def block_mask(block_ids, column_ids, rowblocks, counts, widths):
    slot_total = rowblocks.shape[1]
    owner_node = column_ids // B
    within = column_ids % B
    chosen = owner_node[:, None] == jnp.arange(SNODES, dtype=jnp.int32)[None, :]
    owner_rows = jnp.sum(jnp.where(chosen[:, :, None], rowblocks[None, :, :], 0), axis=1)
    owner_count = jnp.sum(jnp.where(chosen, counts[None, :], 0), axis=1)
    owner_width = jnp.sum(jnp.where(chosen, widths[None, :], 0), axis=1)
    slot_live = jnp.arange(slot_total, dtype=jnp.int32)[None, :] < owner_count[:, None]
    matched = (owner_rows[None, :, :] == block_ids[:, None, None]) & slot_live[None, :, :]
    present = jnp.any(matched, axis=2) & (within < owner_width)[None, :]
    return (present, owner_width, within)


def per_device(ainv, lpanel, dinv, rowblocks, counts, widths):
    row_group = lax.axis_index("prow")
    col_group = lax.axis_index("pcol")
    panel_rows = lpanel.shape[0]
    panel_cols = lpanel.shape[1]
    inverse_rows = ainv.shape[0]
    share_cols = dinv.shape[1]
    row_blocks = panel_rows // B
    col_blocks = inverse_rows // B
    own_ids = row_group * row_blocks + jnp.arange(row_blocks, dtype=jnp.int32)
    own_cols = col_group * panel_cols + jnp.arange(panel_cols, dtype=jnp.int32)
    present, unused_width, unused_within = block_mask(own_ids, own_cols, rowblocks, counts, widths)
    masked = jnp.where(
        present[:, None, :], lpanel.reshape(row_blocks, B, panel_cols), jnp.zeros((), jnp.bfloat16)
    )
    masked = masked.reshape(panel_rows, panel_cols)
    gathered = lax.all_gather(masked, "pcol", axis=1, tiled=True)
    product = jnp.dot(ainv, gathered, preferred_element_type=jnp.float32)
    root_row = col_group * col_blocks // row_blocks
    offset = (col_group * col_blocks - root_row * row_blocks) * B
    own_rows = lax.dynamic_slice_in_dim(gathered, offset, inverse_rows, 0)
    width_cols = max(share_cols, B)
    first_col = row_group * share_cols // width_cols * width_cols
    summed = lax.psum_scatter(
        product.astype(jnp.bfloat16), "prow", scatter_dimension=1, tiled=True
    ).astype(jnp.float32)
    whole_rows = from_root(own_rows, "prow", root_row)
    across = lax.dynamic_slice_in_dim(whole_rows, first_col, width_cols, 1)
    column_ids = row_group * share_cols + jnp.arange(share_cols, dtype=jnp.int32)
    block_ids = col_group * col_blocks + jnp.arange(col_blocks, dtype=jnp.int32)
    kept, owner_width, within = block_mask(block_ids, column_ids, rowblocks, counts, widths)
    negated = jnp.where(
        kept[:, None, :], -summed.reshape(col_blocks, B, share_cols), jnp.zeros((), jnp.float32)
    )
    selected_inverse = negated.reshape(inverse_rows, share_cols).astype(jnp.bfloat16)
    groups = max(1, share_cols // B)
    left_side = across.reshape(inverse_rows, groups, width_cols // groups).astype(jnp.float32)
    right_side = summed.reshape(inverse_rows, groups, share_cols // groups)
    quadratic = jnp.einsum(
        "rnb,rnc->bnc", left_side, right_side, precision=lax.Precision.HIGHEST
    ).reshape(B, share_cols)
    quadratic = lax.psum(quadratic.astype(jnp.bfloat16), "pcol").astype(jnp.float32)
    corner = (jnp.arange(B, dtype=jnp.int32)[:, None] < owner_width[None, :]) & (
        within < owner_width
    )[None, :]
    diagonal_blocks = jnp.where(corner, dinv, jnp.zeros((), jnp.float32)) + quadratic
    return (selected_inverse, diagonal_blocks)


PIECES = 2


def handoff_kernel(sel_in, diag_in, sel_out, diag_out, sel_held, diag_held, in_sem, out_sem):
    reads, writes = [], []
    for k, (src, held, dst) in enumerate([(sel_in, sel_held, sel_out), (diag_in, diag_held, diag_out)]):
        part = src.shape[0] // PIECES
        for i in range(PIECES):
            piece = pl.ds(i * part, part)
            n = k * PIECES + i
            reads.append(pltpu.make_async_copy(src.at[piece], held.at[piece], in_sem.at[n]))
            writes.append(pltpu.make_async_copy(held.at[piece], dst.at[piece], out_sem.at[n]))
    for copy in reads:
        copy.start()
    for read, write in zip(reads, writes):
        read.wait()
        write.start()
    for copy in writes:
        copy.wait()


def level_kernel(
    n_z, n_x,
    a_hbm, lp_hbm, dinv_hbm, rb_hbm, cnt_hbm, wid_hbm,
    sel_ref, diag_ref,
    a_buf, lp_ref, dinv_ref, rb_ref, cnt_ref, wid_ref,
    fbuf, froot, froot_t, pown, pkeep, pair_out, pair_in, cross_out, cross_in, part_out, part_in,
    pall, pbf, pnb, dpart, drec, dall,
    late_keep, late_out, late_in, late_sum, late_cin, late_dpart,
    in_sem, a_sem, fsend, frecv, rsend, rrecv,
    pair_s, pair_r, cross_s, cross_r, part_s, part_r, xsem_s, xsem_r,
    d1_s, d1_r, d2_s, d2_r, late_ps, late_pr, late_ss, late_cr, late_ds,
):
    p = lax.axis_index("prow")
    c = lax.axis_index("pcol")
    z = lax.div(c, n_x)
    x = lax.rem(c, n_x)
    xo = 1 - x
    y = lax.div(p, 2)
    core = lax.rem(p, 2)
    mate = 2 * y + 1 - core
    rows = a_hbm.shape[0]
    H = 128
    halves = B // H
    slots = rb_ref.shape[1]
    row_blocks = lp_ref.shape[0] // B
    out_blocks = rows // B
    slice_rows = B // n_z

    fetches = [
        pltpu.make_async_copy(src, dst, in_sem.at[i])
        for i, (src, dst) in enumerate(
            [
                (rb_hbm, rb_ref), (cnt_hbm, cnt_ref), (wid_hbm, wid_ref),
                (lp_hbm, lp_ref), (a_hbm, a_buf.at[0]), (dinv_hbm, dinv_ref),
            ]
        )
    ]
    for fetch in fetches:
        fetch.start()

    def live(block, node):
        count = cnt_ref[node]
        hit = jnp.int32(0)
        for i in range(slots):
            hit += jnp.where((rb_ref[node, i] == block) & (i < count), 1, 0)
        return hit

    def remote(src, dst, s_sem, r_sem, prow, pcol):
        return pltpu.make_async_remote_copy(
            src_ref=src, dst_ref=dst, send_sem=s_sem, recv_sem=r_sem,
            device_id=(prow, pcol), device_id_type=MESH,
        )

    barrier = pltpu.get_barrier_semaphore()
    spot = z * n_z + p
    for d in range(1, n_z * n_z):
        q = lax.rem(spot + d, n_z * n_z)
        pl.semaphore_signal(
            barrier, inc=1, device_id=(lax.rem(q, n_z), lax.div(q, n_z) * n_x + x), device_id_type=MESH
        )
    for d in range(n_z):
        pl.semaphore_signal(barrier, inc=1, device_id=(p, d * n_x + xo), device_id_type=MESH)

    a_copy = remote(a_hbm, a_buf.at[1], a_sem.at[0], a_sem.at[1], p, z * n_x + xo)

    def f_copy(s, h, way):
        return remote(
            fbuf.at[s, h], fbuf.at[s, h], fsend.at[way, s, h], frecv.at[s, h],
            p, (z + (1 - 2 * way)) * n_x + x,
        )

    def root_copy(s, h):
        return remote(fbuf.at[s, h], froot.at[h], rsend.at[s, h], rrecv.at[h], s, c)

    def part_copy(r, h):
        return remote(part_out.at[r, h], part_in.at[r, h], part_s.at[r, h], part_r.at[r, h], mate, c)

    def pair_copy(e, h):
        return remote(pair_out.at[e, h], pair_in.at[e, h], pair_s.at[e, h], pair_r.at[e, h], mate, c)

    def cross_copy(e, r, h):
        return remote(
            cross_out.at[e, h], cross_in.at[r, h], cross_s.at[e, h], cross_r.at[r, h], 2 * (1 - y) + e, c
        )

    def x_copy(h):
        return remote(pbf.at[h], pnb.at[h], xsem_s.at[h], xsem_r.at[h], p, z * n_x + xo)

    def partial(s, r, h):
        value = jnp.dot(a_buf[r], fbuf[s, h], preferred_element_type=jnp.float32)
        e = lax.rem(s, 2)
        same = lax.div(s, 2) == y

        @pl.when(same & (s == p))
        def _():
            pown[r, h] = value

        @pl.when(same & (s != p))
        def _():
            part_out[r, h] = value.astype(jnp.bfloat16)
            part_copy(r, h).start()

        @pl.when(jnp.logical_not(same) & (r == core))
        def _():
            pkeep[e, h] = value

        @pl.when(jnp.logical_not(same) & (r != core))
        def _():
            pair_out[e, h] = value.astype(jnp.bfloat16)
            pair_copy(e, h).start()

    def finalize(s, r, h):
        e = lax.rem(s, 2)

        @pl.when((lax.div(s, 2) != y) & (r == core))
        def _():
            pair_copy(e, h).wait_recv()
            cross_out[e, h] = (pkeep[e, h] + pair_in[e, h].astype(jnp.float32)).astype(jnp.bfloat16)
            cross_copy(e, r, h).start()

    def root_send(s, h):
        @pl.when(p == z)
        def _():
            @pl.when(s != z)
            def _():
                root_copy(s, h).start()

            @pl.when(s == z)
            def _():
                froot[h] = fbuf[s, h]

    for fetch in fetches[:4]:
        fetch.wait()
    width = wid_ref[c]
    limits = [jnp.where(live(p * row_blocks + b, c) > 0, width, 0) for b in range(row_blocks)]
    for h in range(halves):
        for b in range(row_blocks):
            cols = lax.broadcasted_iota(jnp.int32, (B, H), 1) + h * H
            value = lp_ref[b * B:(b + 1) * B, h * H:(h + 1) * H].astype(jnp.float32)
            fbuf[z, h, b * B:(b + 1) * B, :] = jnp.where(cols < limits[b], value, 0.0).astype(jnp.bfloat16)
        if h == 0:
            pl.semaphore_wait(barrier, n_z * n_z - 1 + n_z)
            a_copy.start()

        @pl.when(z < n_z - 1)
        def _():
            f_copy(z, h, 0).start()

        @pl.when(z > 0)
        def _():
            f_copy(z, h, 1).start()
    for fetch in fetches[4:]:
        fetch.wait()

    def both(j, act):
        t = lax.div(j, halves)
        h = lax.rem(j, halves)
        for way in range(2):
            s = z - t * (1 - 2 * way)
            valid = (s >= 0) & (s < n_z)
            if way == 1:
                valid = valid & (t > 0)

            @pl.when(valid)
            def _():
                act(t, h, way, s)

    def arrive(t, h, way, s):
        @pl.when(t > 0)
        def _():
            f_copy(s, h, way).wait_recv()
            onward = z + (1 - 2 * way)

            @pl.when((onward >= 0) & (onward < n_z))
            def _():
                f_copy(s, h, way).start()

        @pl.when(t < n_z - 1)
        def _():
            root_send(s, h)

    def first(j, carry):
        @pl.when(j < early)
        def _():
            both(j, arrive)

        @pl.when(j > 0)
        def _():
            both(j - 1, lambda t, h, way, s: finalize(s, 0, h))

        @pl.when(j < early)
        def _():
            both(j, lambda t, h, way, s: partial(s, 0, h))

        return carry

    early = (n_z - 1) * halves
    lax.fori_loop(0, early + 1, first, 0)
    a_copy.wait_recv()

    def second(j, carry):
        @pl.when(j < early)
        def _():
            both(j, lambda t, h, way, s: partial(s, 1, h))

        @pl.when(j > 0)
        def _():
            both(j - 1, lambda t, h, way, s: finalize(s, 1, h))

        return carry

    lax.fori_loop(0, early + 1, second, 0)

    late = n_z - 1 - z
    at_end = (z == 0) | (z == n_z - 1)
    late_owner = at_end & (p == late)
    late_root = at_end & (p == z)

    def late_pair(h):
        return remote(late_out.at[h], late_in.at[h], late_ps.at[h], late_pr.at[h], mate, c)

    def late_copy(h, i, to):
        return remote(late_sum.at[h], late_cin.at[y, core, h], late_ss.at[i, h], late_cr.at[y, core, h], to, c)

    def third_act(t, h, way, s):
        arrive(t, h, way, s)

        def each(i, carry):
            value = jnp.dot(a_buf[jnp.where(i == 0, 1 - core, core)], fbuf[s, h], preferred_element_type=jnp.float32)

            @pl.when(i == 0)
            def _():
                late_out[h] = value.astype(jnp.bfloat16)
                late_pair(h).start()

            @pl.when(i == 1)
            def _():
                late_keep[h] = value

            return carry

        lax.fori_loop(0, 2, each, 0)
        late_pair(h).wait_recv()
        value = (late_keep[h] + late_in[h].astype(jnp.float32)).astype(jnp.bfloat16)
        late_sum[h] = value

        @pl.when((p == z) | (p == late))
        def _():
            late_cin[y, core, h] = value

        @pl.when(p != z)
        def _():
            late_copy(h, 0, z).start()

        @pl.when(p != late)
        def _():
            late_copy(h, 1, late).start()

    def late_total(r, h):
        for g in range(2):
            @pl.when(2 * g + r != p)
            def _():
                remote(
                    late_sum.at[h], late_cin.at[g, r, h], late_ss.at[0, h], late_cr.at[g, r, h], p, c
                ).wait_recv()
        return late_cin[0, r, h].astype(jnp.float32) + late_cin[1, r, h].astype(jnp.float32)

    def third(j, carry):
        both(j, third_act)
        return carry

    lax.fori_loop(early, early + halves, third, 0)

    def total(r, h):
        part_copy(r, h).wait_recv()
        cross_copy(core, r, h).wait_recv()
        return pown[r, h] + part_in[r, h].astype(jnp.float32) + cross_in[r, h].astype(jnp.float32)

    signs = [
        [jnp.where(live(c * out_blocks + b, 2 * p + (x if w == 0 else xo)) > 0, -1.0, 0.0) for b in range(out_blocks)]
        for w in range(2)
    ]

    def write(value, w, h):
        node = x if w == 0 else xo
        lane = pl.multiple_of(node * B + h * H, H)
        for b in range(out_blocks):
            sel_ref[b * B:(b + 1) * B, pl.ds(lane, H)] = (value[b * B:(b + 1) * B] * signs[w][b]).astype(jnp.bfloat16)

    starts = [pl.multiple_of(x * rows, rows), pl.multiple_of(xo * rows, rows)]

    def d1_copy(to, own):
        return remote(
            dpart.at[pl.ds(pl.multiple_of(to * slice_rows, slice_rows), slice_rows)], drec.at[own],
            d1_s.at[to], d1_r.at[own], p, to * n_x + x,
        )

    def late_d1(to):
        return remote(
            late_dpart.at[to * slice_rows:(to + 1) * slice_rows], drec.at[z],
            late_ds.at[to], d1_r.at[z], late, to * n_x + x,
        )

    @pl.when(jnp.logical_not(late_owner))
    def _():
        for h in range(halves):
            @pl.when(p != z)
            def _():
                root_copy(p, h).wait_recv()
            froot_t[h * H:(h + 1) * H, :] = jnp.transpose(froot[h])
            value = total(1, h).astype(jnp.bfloat16)
            pbf[h] = value
            x_copy(h).start()
            pall[pl.ds(starts[1], rows), h * H:(h + 1) * H] = value
            value = total(0, h)
            pall[pl.ds(starts[0], rows), h * H:(h + 1) * H] = value.astype(jnp.bfloat16)
            write(value, 0, h)
        dpart[...] = jnp.dot(froot_t[...], pall[...], preferred_element_type=jnp.float32).astype(jnp.bfloat16)
        drec[z] = dpart[pl.ds(pl.multiple_of(z * slice_rows, slice_rows), slice_rows)]
        for d in range(1, n_z):
            d1_copy(lax.rem(z + d, n_z), z).start()

    @pl.when(late_owner)
    def _():
        for h in range(halves):
            pbf[h] = late_total(1, h).astype(jnp.bfloat16)
            x_copy(h).start()
            write(late_total(0, h), 0, h)

    @pl.when(late_root)
    def _():
        for h in range(halves):
            froot_t[h * H:(h + 1) * H, :] = jnp.transpose(fbuf[late, h])
        for h in range(halves):
            for r in range(2):
                pall[pl.ds(starts[r], rows), h * H:(h + 1) * H] = late_total(r, h).astype(jnp.bfloat16)
        late_dpart[...] = jnp.dot(
            froot_t[...], pall[...], preferred_element_type=jnp.float32
        ).astype(jnp.bfloat16)
        for to in range(n_z):
            late_d1(to).start()

    value = jnp.zeros((slice_rows, B), jnp.float32)
    for q in range(n_z):
        @pl.when((q != z) | late_owner)
        def _():
            d1_copy(q, q).wait_recv()
        value = value + drec[q].astype(jnp.float32)
    dall[c] = value.astype(jnp.bfloat16)

    def d2_copy(to, own):
        return remote(dall.at[own], dall.at[own], d2_s.at[to], d2_r.at[own], p, to)

    for d in range(1, n_z * n_x):
        d2_copy(lax.rem(c + d, n_z * n_x), c).start()

    for h in range(halves):
        x_copy(h).wait_recv()
        write(pnb[h].astype(jnp.float32), 1, h)

    def corner(w, r):
        wide = wid_ref[2 * p + w]
        shape = (slice_rows, B)
        line = lax.broadcasted_iota(jnp.int32, shape, 0) + r * slice_rows
        col = lax.broadcasted_iota(jnp.int32, shape, 1)
        own = dinv_ref[r * slice_rows:(r + 1) * slice_rows, w * B:(w + 1) * B]
        return jnp.where((line < wide) & (col < wide), own, 0.0)

    for d in range(1, n_z * n_x):
        q = lax.rem(c + d, n_z * n_x)
        d2_copy(q, q).wait_recv()
    for r in range(n_z):
        for w in range(n_x):
            diag_ref[r * slice_rows:(r + 1) * slice_rows, w * B:(w + 1) * B] = (
                corner(w, r) + dall[r * n_x + w].astype(jnp.float32)
            )

    a_copy.wait_send()
    for h in range(halves):
        x_copy(h).wait_send()
        @pl.when(at_end)
        def _():
            late_pair(h).wait_send()

            @pl.when(p != z)
            def _():
                late_copy(h, 0, z).wait_send()

            @pl.when(p != late)
            def _():
                late_copy(h, 1, late).wait_send()

    for s in range(n_z):
        off = (s == late) & at_end
        for h in range(halves):
            @pl.when((s <= z) & (z < n_z - 1))
            def _():
                f_copy(s, h, 0).wait_send()

            @pl.when((s >= z) & (z > 0))
            def _():
                f_copy(s, h, 1).wait_send()

            @pl.when((p == z) & (s != z) & jnp.logical_not(off))
            def _():
                root_copy(s, h).wait_send()

            @pl.when(jnp.logical_not(off) & (s == mate))
            def _():
                for r in range(2):
                    part_copy(r, h).wait_send()

            @pl.when(jnp.logical_not(off) & (lax.div(jnp.int32(s), 2) != y))
            def _():
                pair_copy(s % 2, h).wait_send()
                cross_copy(s % 2, core, h).wait_send()

    @pl.when(jnp.logical_not(late_owner))
    def _():
        for d in range(1, n_z):
            d1_copy(lax.rem(z + d, n_z), z).wait_send()

    @pl.when(late_root)
    def _():
        for to in range(n_z):
            late_d1(to).wait_send()
    for d in range(1, n_z * n_x):
        d2_copy(lax.rem(c + d, n_z * n_x), c).wait_send()


def fused(n_prow, n_pcol, ainv, lpanel, dinv, rowblocks, counts, widths):
    n_z, n_x = n_prow, 2
    rows, depth = ainv.shape
    bf, f32, H = jnp.bfloat16, jnp.float32, 128
    halves = B // H
    vmem = pl.BlockSpec(memory_space=pltpu.VMEM)
    hbm = pl.BlockSpec(memory_space=pltpu.HBM)
    dma = pltpu.SemaphoreType.DMA
    piece = (2, halves, rows, H)
    results = pl.pallas_call(
        functools.partial(level_kernel, n_z, n_x),
        out_shape=(
            jax.ShapeDtypeStruct((rows, dinv.shape[1]), bf),
            jax.ShapeDtypeStruct(dinv.shape, f32),
        ),
        in_specs=[hbm] * 6,
        out_specs=(vmem, vmem),
        scratch_shapes=[
            pltpu.VMEM((2, rows, depth), bf),
            pltpu.VMEM(lpanel.shape, bf),
            pltpu.VMEM(dinv.shape, f32),
            pltpu.SMEM(rowblocks.shape, jnp.int32),
            pltpu.SMEM(counts.shape, jnp.int32),
            pltpu.SMEM(widths.shape, jnp.int32),
            pltpu.VMEM((n_z, halves, depth, H), bf),
            pltpu.VMEM((halves, depth, H), bf),
            pltpu.VMEM((B, depth), bf),
            pltpu.VMEM(piece, f32),
            pltpu.VMEM(piece, f32),
        ]
        + [pltpu.VMEM(piece, bf)] * 6
        + [
            pltpu.VMEM((depth, B), bf),
            pltpu.VMEM((halves, rows, H), bf),
            pltpu.VMEM((halves, rows, H), bf),
            pltpu.VMEM((B, B), bf),
            pltpu.VMEM((n_z, B // n_z, B), bf),
            pltpu.VMEM((n_z * n_x, B // n_z, B), bf),
            pltpu.VMEM((halves, rows, H), f32),
            pltpu.VMEM((halves, rows, H), bf),
            pltpu.VMEM((halves, rows, H), bf),
            pltpu.VMEM((halves, rows, H), bf),
            pltpu.VMEM((2, 2, halves, rows, H), bf),
            pltpu.VMEM((B, B), bf),
            dma((6,)),
            dma((2,)),
            dma((2, n_z, halves)),
            dma((n_z, halves)),
            dma((n_z, halves)),
            dma((halves,)),
        ]
        + [dma((2, halves))] * 6
        + [
            dma((halves,)),
            dma((halves,)),
            dma((n_z,)),
            dma((n_z,)),
            dma((n_z * n_x,)),
            dma((n_z * n_x,)),
            dma((halves,)),
            dma((halves,)),
            dma((2, halves)),
            dma((2, 2, halves)),
            dma((n_z,)),
        ],
        compiler_params=pltpu.CompilerParams(
            collective_id=0, has_side_effects=True, vmem_limit_bytes=60 * 1024 * 1024
        ),
        cost_estimate=pl.CostEstimate(
            flops=2 * rows * depth * SNODES * B, bytes_accessed=4 * 1024 * 1024, transcendentals=0
        ),
    )(ainv, lpanel, dinv, rowblocks, counts, widths)
    anywhere = pl.BlockSpec(memory_space=pl.ANY)
    return pl.pallas_call(
        handoff_kernel,
        out_shape=tuple(jax.ShapeDtypeStruct(r.shape, r.dtype) for r in results),
        in_specs=[anywhere] * 2,
        out_specs=(anywhere, anywhere),
        scratch_shapes=[pltpu.VMEM(r.shape, r.dtype) for r in results]
        + [dma((2 * PIECES,)), dma((2 * PIECES,))],
        compiler_params=pltpu.CompilerParams(vmem_limit_bytes=60 * 1024 * 1024),
    )(*results)


def solution(mesh):
    n_prow, n_pcol = mesh.shape["prow"], mesh.shape["pcol"]

    def step(ainv, lpanel, dinv, rowblocks, counts, widths):
        rows, depth = ainv.shape
        whole = n_prow == 4 and n_pcol == 8 and lpanel.shape[1] == B and dinv.shape[1] == 2 * B
        if whole and depth == 2 * rows and depth == lpanel.shape[0] and rows % B == 0 and B % (16 * n_prow) == 0:
            return fused(n_prow, n_pcol, ainv, lpanel, dinv, rowblocks, counts, widths)
        return per_device(ainv, lpanel, dinv, rowblocks, counts, widths)

    placed = (P("pcol", "prow"), P("prow", "pcol"), P(None, "prow"), P(), P(), P())
    return jax.shard_map(
        step,
        mesh=mesh,
        in_specs=placed,
        out_specs=(P("pcol", "prow"), P(None, "prow")),
        check_vma=False,
    )
```

```python
import functools

import jax
import jax.numpy as jnp
from jax import lax
from jax.experimental import pallas as pl
from jax.experimental.pallas import tpu as pltpu
from jax.sharding import PartitionSpec as P

MESH = pl.DeviceIdType.MESH

B = 256
SNODES = 8


def from_root(value, axis, source):
    kept = jnp.where(lax.axis_index(axis) == source, value, 0).astype(value.dtype)
    return lax.psum(kept, axis)


def block_mask(block_ids, column_ids, rowblocks, counts, widths):
    slot_total = rowblocks.shape[1]
    owner_node = column_ids // B
    within = column_ids % B
    chosen = owner_node[:, None] == jnp.arange(SNODES, dtype=jnp.int32)[None, :]
    owner_rows = jnp.sum(jnp.where(chosen[:, :, None], rowblocks[None, :, :], 0), axis=1)
    owner_count = jnp.sum(jnp.where(chosen, counts[None, :], 0), axis=1)
    owner_width = jnp.sum(jnp.where(chosen, widths[None, :], 0), axis=1)
    slot_live = jnp.arange(slot_total, dtype=jnp.int32)[None, :] < owner_count[:, None]
    matched = (owner_rows[None, :, :] == block_ids[:, None, None]) & slot_live[None, :, :]
    present = jnp.any(matched, axis=2) & (within < owner_width)[None, :]
    return (present, owner_width, within)


def per_device(ainv, lpanel, dinv, rowblocks, counts, widths):
    row_group = lax.axis_index("prow")
    col_group = lax.axis_index("pcol")
    panel_rows = lpanel.shape[0]
    panel_cols = lpanel.shape[1]
    inverse_rows = ainv.shape[0]
    share_cols = dinv.shape[1]
    row_blocks = panel_rows // B
    col_blocks = inverse_rows // B
    own_ids = row_group * row_blocks + jnp.arange(row_blocks, dtype=jnp.int32)
    own_cols = col_group * panel_cols + jnp.arange(panel_cols, dtype=jnp.int32)
    present, unused_width, unused_within = block_mask(own_ids, own_cols, rowblocks, counts, widths)
    masked = jnp.where(
        present[:, None, :], lpanel.reshape(row_blocks, B, panel_cols), jnp.zeros((), jnp.bfloat16)
    )
    masked = masked.reshape(panel_rows, panel_cols)
    gathered = lax.all_gather(masked, "pcol", axis=1, tiled=True)
    product = jnp.dot(ainv, gathered, preferred_element_type=jnp.float32)
    root_row = col_group * col_blocks // row_blocks
    offset = (col_group * col_blocks - root_row * row_blocks) * B
    own_rows = lax.dynamic_slice_in_dim(gathered, offset, inverse_rows, 0)
    width_cols = max(share_cols, B)
    first_col = row_group * share_cols // width_cols * width_cols
    summed = lax.psum_scatter(
        product.astype(jnp.bfloat16), "prow", scatter_dimension=1, tiled=True
    ).astype(jnp.float32)
    whole_rows = from_root(own_rows, "prow", root_row)
    across = lax.dynamic_slice_in_dim(whole_rows, first_col, width_cols, 1)
    column_ids = row_group * share_cols + jnp.arange(share_cols, dtype=jnp.int32)
    block_ids = col_group * col_blocks + jnp.arange(col_blocks, dtype=jnp.int32)
    kept, owner_width, within = block_mask(block_ids, column_ids, rowblocks, counts, widths)
    negated = jnp.where(
        kept[:, None, :], -summed.reshape(col_blocks, B, share_cols), jnp.zeros((), jnp.float32)
    )
    selected_inverse = negated.reshape(inverse_rows, share_cols).astype(jnp.bfloat16)
    groups = max(1, share_cols // B)
    left_side = across.reshape(inverse_rows, groups, width_cols // groups).astype(jnp.float32)
    right_side = summed.reshape(inverse_rows, groups, share_cols // groups)
    quadratic = jnp.einsum(
        "rnb,rnc->bnc", left_side, right_side, precision=lax.Precision.HIGHEST
    ).reshape(B, share_cols)
    quadratic = lax.psum(quadratic.astype(jnp.bfloat16), "pcol").astype(jnp.float32)
    corner = (jnp.arange(B, dtype=jnp.int32)[:, None] < owner_width[None, :]) & (
        within < owner_width
    )[None, :]
    diagonal_blocks = jnp.where(corner, dinv, jnp.zeros((), jnp.float32)) + quadratic
    return (selected_inverse, diagonal_blocks)


PIECES = 2


def handoff_kernel(sel_in, diag_in, sel_out, diag_out, sel_held, diag_held, in_sem, out_sem):
    reads, writes = [], []
    for k, (src, held, dst) in enumerate([(sel_in, sel_held, sel_out), (diag_in, diag_held, diag_out)]):
        part = src.shape[0] // PIECES
        for i in range(PIECES):
            piece = pl.ds(i * part, part)
            n = k * PIECES + i
            reads.append(pltpu.make_async_copy(src.at[piece], held.at[piece], in_sem.at[n]))
            writes.append(pltpu.make_async_copy(held.at[piece], dst.at[piece], out_sem.at[n]))
    for copy in reads:
        copy.start()
    for read, write in zip(reads, writes):
        read.wait()
        write.start()
    for copy in writes:
        copy.wait()


def level_kernel(
    n_z, n_x,
    a_hbm, lp_hbm, dinv_hbm, rb_hbm, cnt_hbm, wid_hbm,
    sel_hbm, diag_hbm,
    sel_ref, diag_ref, a_buf, lp_ref, dinv_ref, rb_ref, cnt_ref, wid_ref,
    fbuf, froot, froot_t, pown, pkeep, pair_out, pair_in, cross_out, cross_in, part_out, part_in,
    pall, pbf, pnb, dpart, drec, dall,
    late_keep, late_out, late_in, late_sum, late_cin, late_dpart,
    in_sem, a_sem, fsend, frecv, rsend, rrecv,
    pair_s, pair_r, cross_s, cross_r, part_s, part_r, xsem_s, xsem_r,
    d1_s, d1_r, d2_s, d2_r, late_ps, late_pr, late_ss, late_cr, late_ds, out_s,
):
    p = lax.axis_index("prow")
    c = lax.axis_index("pcol")
    z = lax.div(c, n_x)
    x = lax.rem(c, n_x)
    xo = 1 - x
    y = lax.div(p, 2)
    core = lax.rem(p, 2)
    mate = 2 * y + 1 - core
    rows = a_hbm.shape[0]
    H = 128
    halves = B // H
    slots = rb_ref.shape[1]
    row_blocks = lp_ref.shape[0] // B
    out_blocks = rows // B
    slice_rows = B // n_z

    fetches = [
        pltpu.make_async_copy(src, dst, in_sem.at[i])
        for i, (src, dst) in enumerate(
            [
                (rb_hbm, rb_ref), (cnt_hbm, cnt_ref), (wid_hbm, wid_ref),
                (lp_hbm, lp_ref), (a_hbm, a_buf.at[0]), (dinv_hbm, dinv_ref),
            ]
        )
    ]
    for fetch in fetches:
        fetch.start()

    def live(block, node):
        count = cnt_ref[node]
        hit = jnp.int32(0)
        for i in range(slots):
            hit += jnp.where((rb_ref[node, i] == block) & (i < count), 1, 0)
        return hit

    def remote(src, dst, s_sem, r_sem, prow, pcol):
        return pltpu.make_async_remote_copy(
            src_ref=src, dst_ref=dst, send_sem=s_sem, recv_sem=r_sem,
            device_id=(prow, pcol), device_id_type=MESH,
        )

    barrier = pltpu.get_barrier_semaphore()
    spot = z * n_z + p
    for d in range(1, n_z * n_z):
        q = lax.rem(spot + d, n_z * n_z)
        pl.semaphore_signal(
            barrier, inc=1, device_id=(lax.rem(q, n_z), lax.div(q, n_z) * n_x + x), device_id_type=MESH
        )
    for d in range(n_z):
        pl.semaphore_signal(barrier, inc=1, device_id=(p, d * n_x + xo), device_id_type=MESH)

    a_copy = remote(a_hbm, a_buf.at[1], a_sem.at[0], a_sem.at[1], p, z * n_x + xo)

    def f_copy(s, h, way):
        return remote(
            fbuf.at[s, h], fbuf.at[s, h], fsend.at[way, s, h], frecv.at[s, h],
            p, (z + (1 - 2 * way)) * n_x + x,
        )

    def root_copy(s, h):
        return remote(fbuf.at[s, h], froot.at[h], rsend.at[s, h], rrecv.at[h], s, c)

    def part_copy(r, h):
        return remote(part_out.at[r, h], part_in.at[r, h], part_s.at[r, h], part_r.at[r, h], mate, c)

    def pair_copy(e, h):
        return remote(pair_out.at[e, h], pair_in.at[e, h], pair_s.at[e, h], pair_r.at[e, h], mate, c)

    def cross_copy(e, r, h):
        return remote(
            cross_out.at[e, h], cross_in.at[r, h], cross_s.at[e, h], cross_r.at[r, h], 2 * (1 - y) + e, c
        )

    def x_copy(h):
        return remote(pbf.at[h], pnb.at[h], xsem_s.at[h], xsem_r.at[h], p, z * n_x + xo)

    def partial(s, r, h):
        value = jnp.dot(a_buf[r], fbuf[s, h], preferred_element_type=jnp.float32)
        e = lax.rem(s, 2)
        same = lax.div(s, 2) == y

        @pl.when(same & (s == p))
        def _():
            pown[r, h] = value

        @pl.when(same & (s != p))
        def _():
            part_out[r, h] = value.astype(jnp.bfloat16)
            part_copy(r, h).start()

        @pl.when(jnp.logical_not(same) & (r == core))
        def _():
            pkeep[e, h] = value

        @pl.when(jnp.logical_not(same) & (r != core))
        def _():
            pair_out[e, h] = value.astype(jnp.bfloat16)
            pair_copy(e, h).start()

    def finalize(s, r, h):
        e = lax.rem(s, 2)

        @pl.when((lax.div(s, 2) != y) & (r == core))
        def _():
            pair_copy(e, h).wait_recv()
            cross_out[e, h] = (pkeep[e, h] + pair_in[e, h].astype(jnp.float32)).astype(jnp.bfloat16)
            cross_copy(e, r, h).start()

    def root_send(s, h):
        @pl.when(p == z)
        def _():
            @pl.when(s != z)
            def _():
                root_copy(s, h).start()

            @pl.when(s == z)
            def _():
                froot[h] = fbuf[s, h]

    for fetch in fetches[:4]:
        fetch.wait()
    width = wid_ref[c]
    limits = [jnp.where(live(p * row_blocks + b, c) > 0, width, 0) for b in range(row_blocks)]
    for h in range(halves):
        for b in range(row_blocks):
            cols = lax.broadcasted_iota(jnp.int32, (B, H), 1) + h * H
            value = lp_ref[b * B:(b + 1) * B, h * H:(h + 1) * H].astype(jnp.float32)
            fbuf[z, h, b * B:(b + 1) * B, :] = jnp.where(cols < limits[b], value, 0.0).astype(jnp.bfloat16)
        if h == 0:
            pl.semaphore_wait(barrier, n_z * n_z - 1 + n_z)
            a_copy.start()

        @pl.when(z < n_z - 1)
        def _():
            f_copy(z, h, 0).start()

        @pl.when(z > 0)
        def _():
            f_copy(z, h, 1).start()
    for fetch in fetches[4:]:
        fetch.wait()

    def both(j, act):
        t = lax.div(j, halves)
        h = lax.rem(j, halves)
        for way in range(2):
            s = z - t * (1 - 2 * way)
            valid = (s >= 0) & (s < n_z)
            if way == 1:
                valid = valid & (t > 0)

            @pl.when(valid)
            def _():
                act(t, h, way, s)

    def arrive(t, h, way, s):
        @pl.when(t > 0)
        def _():
            f_copy(s, h, way).wait_recv()
            onward = z + (1 - 2 * way)

            @pl.when((onward >= 0) & (onward < n_z))
            def _():
                f_copy(s, h, way).start()

        @pl.when(t < n_z - 1)
        def _():
            root_send(s, h)

    def first(j, carry):
        @pl.when(j < early)
        def _():
            both(j, arrive)

        @pl.when(j > 0)
        def _():
            both(j - 1, lambda t, h, way, s: finalize(s, 0, h))

        @pl.when(j < early)
        def _():
            both(j, lambda t, h, way, s: partial(s, 0, h))

        return carry

    early = (n_z - 1) * halves
    lax.fori_loop(0, early + 1, first, 0)
    def sel_copy(w, h):
        lane = pl.multiple_of((x if w == 0 else xo) * B + h * H, H)
        return pltpu.make_async_copy(sel_ref.at[:, pl.ds(lane, H)], sel_hbm.at[:, pl.ds(lane, H)], out_s.at[w, h])

    signs = [
        [jnp.where(live(c * out_blocks + b, 2 * p + (x if w == 0 else xo)) > 0, -1.0, 0.0) for b in range(out_blocks)]
        for w in range(2)
    ]

    def write(value, w, h):
        node = x if w == 0 else xo
        lane = pl.multiple_of(node * B + h * H, H)
        for b in range(out_blocks):
            sel_ref[b * B:(b + 1) * B, pl.ds(lane, H)] = (value[b * B:(b + 1) * B] * signs[w][b]).astype(jnp.bfloat16)
        sel_copy(w, h).start()

    def corner(w, r):
        wide = wid_ref[2 * p + w]
        shape = (slice_rows, B)
        line = lax.broadcasted_iota(jnp.int32, shape, 0) + r * slice_rows
        col = lax.broadcasted_iota(jnp.int32, shape, 1)
        own = dinv_ref[r * slice_rows:(r + 1) * slice_rows, w * B:(w + 1) * B]
        return jnp.where((line < wide) & (col < wide), own, 0.0)

    for r in range(n_z):
        for w in range(n_x):
            diag_ref[r * slice_rows:(r + 1) * slice_rows, w * B:(w + 1) * B] = corner(w, r)
    a_copy.wait_recv()

    def second(j, carry):
        @pl.when(j < early)
        def _():
            both(j, lambda t, h, way, s: partial(s, 1, h))

        @pl.when(j > 0)
        def _():
            both(j - 1, lambda t, h, way, s: finalize(s, 1, h))

        return carry

    lax.fori_loop(0, early + 1, second, 0)

    late = n_z - 1 - z
    at_end = (z == 0) | (z == n_z - 1)
    late_owner = at_end & (p == late)
    late_root = at_end & (p == z)

    def late_pair(h):
        return remote(late_out.at[h], late_in.at[h], late_ps.at[h], late_pr.at[h], mate, c)

    def late_copy(h, i, to):
        return remote(late_sum.at[h], late_cin.at[y, core, h], late_ss.at[i, h], late_cr.at[y, core, h], to, c)

    def third_act(t, h, way, s):
        arrive(t, h, way, s)

        def each(i, carry):
            value = jnp.dot(a_buf[jnp.where(i == 0, 1 - core, core)], fbuf[s, h], preferred_element_type=jnp.float32)

            @pl.when(i == 0)
            def _():
                late_out[h] = value.astype(jnp.bfloat16)
                late_pair(h).start()

            @pl.when(i == 1)
            def _():
                late_keep[h] = value

            return carry

        lax.fori_loop(0, 2, each, 0)
        late_pair(h).wait_recv()
        value = (late_keep[h] + late_in[h].astype(jnp.float32)).astype(jnp.bfloat16)
        late_sum[h] = value

        @pl.when((p == z) | (p == late))
        def _():
            late_cin[y, core, h] = value

        @pl.when(p != z)
        def _():
            late_copy(h, 0, z).start()

        @pl.when(p != late)
        def _():
            late_copy(h, 1, late).start()

    def late_total(r, h):
        for g in range(2):
            @pl.when(2 * g + r != p)
            def _():
                remote(
                    late_sum.at[h], late_cin.at[g, r, h], late_ss.at[0, h], late_cr.at[g, r, h], p, c
                ).wait_recv()
        return late_cin[0, r, h].astype(jnp.float32) + late_cin[1, r, h].astype(jnp.float32)

    def third(j, carry):
        both(j, third_act)
        return carry

    lax.fori_loop(early, early + halves, third, 0)

    def total(r, h):
        part_copy(r, h).wait_recv()
        cross_copy(core, r, h).wait_recv()
        return pown[r, h] + part_in[r, h].astype(jnp.float32) + cross_in[r, h].astype(jnp.float32)

    starts = [pl.multiple_of(x * rows, rows), pl.multiple_of(xo * rows, rows)]

    def d1_copy(to, own, h):
        return remote(
            dpart.at[h, pl.ds(pl.multiple_of(to * slice_rows, slice_rows), slice_rows)], drec.at[own, h],
            d1_s.at[to, h], d1_r.at[own, h], p, to * n_x + x,
        )

    def late_d1(to, h):
        return remote(
            late_dpart.at[h, to * slice_rows:(to + 1) * slice_rows], drec.at[z, h],
            late_ds.at[to, h], d1_r.at[z, h], late, to * n_x + x,
        )

    def diag_half(out, h):
        out[h] = jnp.dot(
            froot_t[...], pall[:, h * H:(h + 1) * H], preferred_element_type=jnp.float32
        ).astype(jnp.bfloat16)

    def late_half(h):
        @pl.when(late_root)
        def _():
            for r in range(2):
                pall[pl.ds(starts[r], rows), h * H:(h + 1) * H] = late_total(r, h).astype(jnp.bfloat16)
            diag_half(late_dpart, h)
            for to in range(n_z):
                late_d1(to, h).start()

    @pl.when(late_root)
    def _():
        for h in range(halves):
            froot_t[h * H:(h + 1) * H, :] = jnp.transpose(fbuf[late, h])

    late_half(0)

    @pl.when(jnp.logical_not(late_owner))
    def _():
        for h in range(halves):
            @pl.when(p != z)
            def _():
                root_copy(p, h).wait_recv()
            froot_t[h * H:(h + 1) * H, :] = jnp.transpose(froot[h])
            value = total(1, h).astype(jnp.bfloat16)
            pbf[h] = value
            x_copy(h).start()
            pall[pl.ds(starts[1], rows), h * H:(h + 1) * H] = value
            value = total(0, h)
            pall[pl.ds(starts[0], rows), h * H:(h + 1) * H] = value.astype(jnp.bfloat16)
            write(value, 0, h)
        for h in range(halves):
            diag_half(dpart, h)
            drec[z, h] = dpart[h, pl.ds(pl.multiple_of(z * slice_rows, slice_rows), slice_rows)]
            for d in range(1, n_z):
                d1_copy(lax.rem(z + d, n_z), z, h).start()

    @pl.when(late_owner)
    def _():
        for h in range(halves):
            pbf[h] = late_total(1, h).astype(jnp.bfloat16)
            x_copy(h).start()
            write(late_total(0, h), 0, h)

    @pl.when(late_root)
    def _():
        for h in range(halves):
            froot_t[h * H:(h + 1) * H, :] = jnp.transpose(fbuf[late, h])

    for h in range(1, halves):
        late_half(h)

    def d2_copy(to, own, h):
        return remote(dall.at[own, h], dall.at[own, h], d2_s.at[to, h], d2_r.at[own, h], p, to)

    for h in range(halves):
        value = jnp.zeros((slice_rows, H), jnp.float32)
        for q in range(n_z):
            @pl.when((q != z) | late_owner)
            def _():
                d1_copy(q, q, h).wait_recv()
            value = value + drec[q, h].astype(jnp.float32)
        dall[c, h] = value.astype(jnp.bfloat16)
        for d in range(1, n_z * n_x):
            d2_copy(lax.rem(c + d, n_z * n_x), c, h).start()

    for h in range(halves):
        x_copy(h).wait_recv()
        write(pnb[h].astype(jnp.float32), 1, h)

    for h in range(halves):
        for d in range(1, n_z * n_x):
            q = lax.rem(c + d, n_z * n_x)
            d2_copy(q, q, h).wait_recv()
    for r in range(n_z):
        for w in range(n_x):
            for h in range(halves):
                diag_ref[r * slice_rows:(r + 1) * slice_rows, w * B + h * H:w * B + (h + 1) * H] += (
                    dall[r * n_x + w, h].astype(jnp.float32)
                )
    diag_copy = pltpu.make_async_copy(diag_ref, diag_hbm, out_s.at[2, 0])
    diag_copy.start()

    a_copy.wait_send()
    for h in range(halves):
        x_copy(h).wait_send()
        @pl.when(at_end)
        def _():
            late_pair(h).wait_send()

            @pl.when(p != z)
            def _():
                late_copy(h, 0, z).wait_send()

            @pl.when(p != late)
            def _():
                late_copy(h, 1, late).wait_send()

    for s in range(n_z):
        off = (s == late) & at_end
        for h in range(halves):
            @pl.when((s <= z) & (z < n_z - 1))
            def _():
                f_copy(s, h, 0).wait_send()

            @pl.when((s >= z) & (z > 0))
            def _():
                f_copy(s, h, 1).wait_send()

            @pl.when((p == z) & (s != z) & jnp.logical_not(off))
            def _():
                root_copy(s, h).wait_send()

            @pl.when(jnp.logical_not(off) & (s == mate))
            def _():
                for r in range(2):
                    part_copy(r, h).wait_send()

            @pl.when(jnp.logical_not(off) & (lax.div(jnp.int32(s), 2) != y))
            def _():
                pair_copy(s % 2, h).wait_send()
                cross_copy(s % 2, core, h).wait_send()

    for h in range(halves):
        @pl.when(jnp.logical_not(late_owner))
        def _():
            for d in range(1, n_z):
                d1_copy(lax.rem(z + d, n_z), z, h).wait_send()

        @pl.when(late_root)
        def _():
            for to in range(n_z):
                late_d1(to, h).wait_send()

        for d in range(1, n_z * n_x):
            d2_copy(lax.rem(c + d, n_z * n_x), c, h).wait_send()
        for w in range(2):
            sel_copy(w, h).wait()
    diag_copy.wait()


def fused(n_prow, n_pcol, ainv, lpanel, dinv, rowblocks, counts, widths):
    n_z, n_x = n_prow, 2
    rows, depth = ainv.shape
    bf, f32, H = jnp.bfloat16, jnp.float32, 128
    halves = B // H
    hbm = pl.BlockSpec(memory_space=pltpu.HBM)
    dma = pltpu.SemaphoreType.DMA
    piece = (2, halves, rows, H)
    results = pl.pallas_call(
        functools.partial(level_kernel, n_z, n_x),
        out_shape=(
            jax.ShapeDtypeStruct((rows, dinv.shape[1]), bf),
            jax.ShapeDtypeStruct(dinv.shape, f32),
        ),
        in_specs=[hbm] * 6,
        out_specs=(hbm, hbm),
        scratch_shapes=[
            pltpu.VMEM((rows, dinv.shape[1]), bf),
            pltpu.VMEM(dinv.shape, f32),
            pltpu.VMEM((2, rows, depth), bf),
            pltpu.VMEM(lpanel.shape, bf),
            pltpu.VMEM(dinv.shape, f32),
            pltpu.SMEM(rowblocks.shape, jnp.int32),
            pltpu.SMEM(counts.shape, jnp.int32),
            pltpu.SMEM(widths.shape, jnp.int32),
            pltpu.VMEM((n_z, halves, depth, H), bf),
            pltpu.VMEM((halves, depth, H), bf),
            pltpu.VMEM((B, depth), bf),
            pltpu.VMEM(piece, f32),
            pltpu.VMEM(piece, f32),
        ]
        + [pltpu.VMEM(piece, bf)] * 6
        + [
            pltpu.VMEM((depth, B), bf),
            pltpu.VMEM((halves, rows, H), bf),
            pltpu.VMEM((halves, rows, H), bf),
            pltpu.VMEM((halves, B, H), bf),
            pltpu.VMEM((n_z, halves, B // n_z, H), bf),
            pltpu.VMEM((n_z * n_x, halves, B // n_z, H), bf),
            pltpu.VMEM((halves, rows, H), f32),
            pltpu.VMEM((halves, rows, H), bf),
            pltpu.VMEM((halves, rows, H), bf),
            pltpu.VMEM((halves, rows, H), bf),
            pltpu.VMEM((2, 2, halves, rows, H), bf),
            pltpu.VMEM((halves, B, H), bf),
            dma((6,)),
            dma((2,)),
            dma((2, n_z, halves)),
            dma((n_z, halves)),
            dma((n_z, halves)),
            dma((halves,)),
        ]
        + [dma((2, halves))] * 6
        + [
            dma((halves,)),
            dma((halves,)),
            dma((n_z, halves)),
            dma((n_z, halves)),
            dma((n_z * n_x, halves)),
            dma((n_z * n_x, halves)),
            dma((halves,)),
            dma((halves,)),
            dma((2, halves)),
            dma((2, 2, halves)),
            dma((n_z, halves)),
            dma((3, halves)),
        ],
        compiler_params=pltpu.CompilerParams(
            collective_id=0, has_side_effects=True, vmem_limit_bytes=60 * 1024 * 1024
        ),
        cost_estimate=pl.CostEstimate(
            flops=2 * rows * depth * SNODES * B, bytes_accessed=4 * 1024 * 1024, transcendentals=0
        ),
    )(ainv, lpanel, dinv, rowblocks, counts, widths)
    anywhere = pl.BlockSpec(memory_space=pl.ANY)
    return pl.pallas_call(
        handoff_kernel,
        out_shape=tuple(jax.ShapeDtypeStruct(r.shape, r.dtype) for r in results),
        in_specs=[anywhere] * 2,
        out_specs=(anywhere, anywhere),
        scratch_shapes=[pltpu.VMEM(r.shape, r.dtype) for r in results]
        + [dma((2 * PIECES,)), dma((2 * PIECES,))],
        compiler_params=pltpu.CompilerParams(vmem_limit_bytes=60 * 1024 * 1024),
    )(*results)


def solution(mesh):
    n_prow, n_pcol = mesh.shape["prow"], mesh.shape["pcol"]

    def step(ainv, lpanel, dinv, rowblocks, counts, widths):
        rows, depth = ainv.shape
        whole = n_prow == 4 and n_pcol == 8 and lpanel.shape[1] == B and dinv.shape[1] == 2 * B
        if whole and depth == 2 * rows and depth == lpanel.shape[0] and rows % B == 0 and B % (16 * n_prow) == 0:
            return fused(n_prow, n_pcol, ainv, lpanel, dinv, rowblocks, counts, widths)
        return per_device(ainv, lpanel, dinv, rowblocks, counts, widths)

    placed = (P("pcol", "prow"), P("prow", "pcol"), P(None, "prow"), P(), P(), P())
    return jax.shard_map(
        step,
        mesh=mesh,
        in_specs=placed,
        out_specs=(P("pcol", "prow"), P(None, "prow")),
        check_vma=False,
    )
```

```python
import functools

import jax
import jax.numpy as jnp
from jax import lax
from jax.experimental import pallas as pl
from jax.experimental.pallas import tpu as pltpu
from jax.sharding import PartitionSpec as P

MESH = pl.DeviceIdType.MESH

B = 256
SNODES = 8


def from_root(value, axis, source):
    kept = jnp.where(lax.axis_index(axis) == source, value, 0).astype(value.dtype)
    return lax.psum(kept, axis)


def block_mask(block_ids, column_ids, rowblocks, counts, widths):
    slot_total = rowblocks.shape[1]
    owner_node = column_ids // B
    within = column_ids % B
    chosen = owner_node[:, None] == jnp.arange(SNODES, dtype=jnp.int32)[None, :]
    owner_rows = jnp.sum(jnp.where(chosen[:, :, None], rowblocks[None, :, :], 0), axis=1)
    owner_count = jnp.sum(jnp.where(chosen, counts[None, :], 0), axis=1)
    owner_width = jnp.sum(jnp.where(chosen, widths[None, :], 0), axis=1)
    slot_live = jnp.arange(slot_total, dtype=jnp.int32)[None, :] < owner_count[:, None]
    matched = (owner_rows[None, :, :] == block_ids[:, None, None]) & slot_live[None, :, :]
    present = jnp.any(matched, axis=2) & (within < owner_width)[None, :]
    return (present, owner_width, within)


def per_device(ainv, lpanel, dinv, rowblocks, counts, widths):
    row_group = lax.axis_index("prow")
    col_group = lax.axis_index("pcol")
    panel_rows = lpanel.shape[0]
    panel_cols = lpanel.shape[1]
    inverse_rows = ainv.shape[0]
    share_cols = dinv.shape[1]
    row_blocks = panel_rows // B
    col_blocks = inverse_rows // B
    own_ids = row_group * row_blocks + jnp.arange(row_blocks, dtype=jnp.int32)
    own_cols = col_group * panel_cols + jnp.arange(panel_cols, dtype=jnp.int32)
    present, unused_width, unused_within = block_mask(own_ids, own_cols, rowblocks, counts, widths)
    masked = jnp.where(
        present[:, None, :], lpanel.reshape(row_blocks, B, panel_cols), jnp.zeros((), jnp.bfloat16)
    )
    masked = masked.reshape(panel_rows, panel_cols)
    gathered = lax.all_gather(masked, "pcol", axis=1, tiled=True)
    product = jnp.dot(ainv, gathered, preferred_element_type=jnp.float32)
    root_row = col_group * col_blocks // row_blocks
    offset = (col_group * col_blocks - root_row * row_blocks) * B
    own_rows = lax.dynamic_slice_in_dim(gathered, offset, inverse_rows, 0)
    width_cols = max(share_cols, B)
    first_col = row_group * share_cols // width_cols * width_cols
    summed = lax.psum_scatter(
        product.astype(jnp.bfloat16), "prow", scatter_dimension=1, tiled=True
    ).astype(jnp.float32)
    whole_rows = from_root(own_rows, "prow", root_row)
    across = lax.dynamic_slice_in_dim(whole_rows, first_col, width_cols, 1)
    column_ids = row_group * share_cols + jnp.arange(share_cols, dtype=jnp.int32)
    block_ids = col_group * col_blocks + jnp.arange(col_blocks, dtype=jnp.int32)
    kept, owner_width, within = block_mask(block_ids, column_ids, rowblocks, counts, widths)
    negated = jnp.where(
        kept[:, None, :], -summed.reshape(col_blocks, B, share_cols), jnp.zeros((), jnp.float32)
    )
    selected_inverse = negated.reshape(inverse_rows, share_cols).astype(jnp.bfloat16)
    groups = max(1, share_cols // B)
    left_side = across.reshape(inverse_rows, groups, width_cols // groups).astype(jnp.float32)
    right_side = summed.reshape(inverse_rows, groups, share_cols // groups)
    quadratic = jnp.einsum(
        "rnb,rnc->bnc", left_side, right_side, precision=lax.Precision.HIGHEST
    ).reshape(B, share_cols)
    quadratic = lax.psum(quadratic.astype(jnp.bfloat16), "pcol").astype(jnp.float32)
    corner = (jnp.arange(B, dtype=jnp.int32)[:, None] < owner_width[None, :]) & (
        within < owner_width
    )[None, :]
    diagonal_blocks = jnp.where(corner, dinv, jnp.zeros((), jnp.float32)) + quadratic
    return (selected_inverse, diagonal_blocks)


PIECES = 2


def handoff_kernel(sel_in, diag_in, sel_out, diag_out, sel_held, diag_held, in_sem, out_sem):
    reads, writes = [], []
    for k, (src, held, dst) in enumerate([(sel_in, sel_held, sel_out), (diag_in, diag_held, diag_out)]):
        part = src.shape[0] // PIECES
        for i in range(PIECES):
            piece = pl.ds(i * part, part)
            n = k * PIECES + i
            reads.append(pltpu.make_async_copy(src.at[piece], held.at[piece], in_sem.at[n]))
            writes.append(pltpu.make_async_copy(held.at[piece], dst.at[piece], out_sem.at[n]))
    for copy in reads:
        copy.start()
    for read, write in zip(reads, writes):
        read.wait()
        write.start()
    for copy in writes:
        copy.wait()


def level_kernel(
    n_z, n_x,
    a_hbm, lp_hbm, dinv_hbm, rb_hbm, cnt_hbm, wid_hbm,
    sel_hbm, diag_hbm,
    sel_ref, diag_ref, a_buf, lp_ref, dinv_ref, rb_ref, cnt_ref, wid_ref,
    fbuf, froot, froot_t, pown, pkeep, pair_out, pair_in, cross_out, cross_in, part_out, part_in,
    pall, pbf, pnb, dpart, drec, dall,
    late_keep, late_out, late_in, late_sum, late_cin, late_dpart,
    in_sem, a_sem, fsend, frecv, rsend, rrecv,
    pair_s, pair_r, cross_s, cross_r, part_s, part_r, xsem_s, xsem_r,
    d1_s, d1_r, d2_s, d2_r, late_ps, late_pr, late_ss, late_cr, late_ds, out_s,
):
    p = lax.axis_index("prow")
    c = lax.axis_index("pcol")
    z = lax.div(c, n_x)
    x = lax.rem(c, n_x)
    xo = 1 - x
    y = lax.div(p, 2)
    core = lax.rem(p, 2)
    mate = 2 * y + 1 - core
    rows = a_hbm.shape[0]
    H = 128
    halves = B // H
    slots = rb_ref.shape[1]
    row_blocks = lp_ref.shape[0] // B
    out_blocks = rows // B
    slice_rows = B // n_z

    fetches = [
        pltpu.make_async_copy(src, dst, in_sem.at[i])
        for i, (src, dst) in enumerate(
            [
                (rb_hbm, rb_ref), (cnt_hbm, cnt_ref), (wid_hbm, wid_ref),
                (lp_hbm, lp_ref), (a_hbm, a_buf.at[0]), (dinv_hbm, dinv_ref),
            ]
        )
    ]
    for fetch in fetches:
        fetch.start()

    def live(block, node):
        count = cnt_ref[node]
        hit = jnp.int32(0)
        for i in range(slots):
            hit += jnp.where((rb_ref[node, i] == block) & (i < count), 1, 0)
        return hit

    def remote(src, dst, s_sem, r_sem, prow, pcol):
        return pltpu.make_async_remote_copy(
            src_ref=src, dst_ref=dst, send_sem=s_sem, recv_sem=r_sem,
            device_id=(prow, pcol), device_id_type=MESH,
        )

    barrier = pltpu.get_barrier_semaphore()
    spot = z * n_z + p
    for d in range(1, n_z * n_z):
        q = lax.rem(spot + d, n_z * n_z)
        pl.semaphore_signal(
            barrier, inc=1, device_id=(lax.rem(q, n_z), lax.div(q, n_z) * n_x + x), device_id_type=MESH
        )
    for d in range(n_z):
        pl.semaphore_signal(barrier, inc=1, device_id=(p, d * n_x + xo), device_id_type=MESH)

    a_copy = remote(a_buf.at[0], a_buf.at[1], a_sem.at[0], a_sem.at[1], p, z * n_x + xo)

    def f_copy(s, h, way):
        return remote(
            fbuf.at[s, h], fbuf.at[s, h], fsend.at[way, s, h], frecv.at[s, h],
            p, (z + (1 - 2 * way)) * n_x + x,
        )

    def root_copy(s, h):
        return remote(fbuf.at[s, h], froot.at[h], rsend.at[s, h], rrecv.at[h], s, c)

    def part_copy(r, h):
        return remote(part_out.at[r, h], part_in.at[r, h], part_s.at[r, h], part_r.at[r, h], mate, c)

    def pair_copy(e, h):
        return remote(pair_out.at[e, h], pair_in.at[e, h], pair_s.at[e, h], pair_r.at[e, h], mate, c)

    def cross_copy(e, r, h):
        return remote(
            cross_out.at[e, h], cross_in.at[r, h], cross_s.at[e, h], cross_r.at[r, h], 2 * (1 - y) + e, c
        )

    def x_copy(h):
        return remote(pbf.at[h], pnb.at[h], xsem_s.at[h], xsem_r.at[h], p, z * n_x + xo)

    def partial(s, r, h):
        value = jnp.dot(a_buf[r], fbuf[s, h], preferred_element_type=jnp.float32)
        e = lax.rem(s, 2)
        same = lax.div(s, 2) == y

        @pl.when(same & (s == p))
        def _():
            pown[r, h] = value

        @pl.when(same & (s != p))
        def _():
            part_out[r, h] = value.astype(jnp.bfloat16)
            part_copy(r, h).start()

        @pl.when(jnp.logical_not(same) & (r == core))
        def _():
            pkeep[e, h] = value

        @pl.when(jnp.logical_not(same) & (r != core))
        def _():
            pair_out[e, h] = value.astype(jnp.bfloat16)
            pair_copy(e, h).start()

    def finalize(s, r, h):
        e = lax.rem(s, 2)

        @pl.when((lax.div(s, 2) != y) & (r == core))
        def _():
            pair_copy(e, h).wait_recv()
            cross_out[e, h] = (pkeep[e, h] + pair_in[e, h].astype(jnp.float32)).astype(jnp.bfloat16)
            cross_copy(e, r, h).start()

    def root_send(s, h):
        @pl.when(p == z)
        def _():
            @pl.when(s != z)
            def _():
                root_copy(s, h).start()

            @pl.when(s == z)
            def _():
                froot[h] = fbuf[s, h]

    for fetch in fetches[:4]:
        fetch.wait()
    width = wid_ref[c]
    limits = [jnp.where(live(p * row_blocks + b, c) > 0, width, 0) for b in range(row_blocks)]
    for h in range(halves):
        for b in range(row_blocks):
            cols = lax.broadcasted_iota(jnp.int32, (B, H), 1) + h * H
            value = lp_ref[b * B:(b + 1) * B, h * H:(h + 1) * H].astype(jnp.float32)
            fbuf[z, h, b * B:(b + 1) * B, :] = jnp.where(cols < limits[b], value, 0.0).astype(jnp.bfloat16)
        if h == 0:
            fetches[4].wait()
            pl.semaphore_wait(barrier, n_z * n_z - 1 + n_z)
            a_copy.start()

        @pl.when(z < n_z - 1)
        def _():
            f_copy(z, h, 0).start()

        @pl.when(z > 0)
        def _():
            f_copy(z, h, 1).start()
    fetches[5].wait()

    def both(j, act):
        t = lax.div(j, halves)
        h = lax.rem(j, halves)
        for way in range(2):
            s = z - t * (1 - 2 * way)
            valid = (s >= 0) & (s < n_z)
            if way == 1:
                valid = valid & (t > 0)

            @pl.when(valid)
            def _():
                act(t, h, way, s)

    def arrive(t, h, way, s):
        @pl.when(t > 0)
        def _():
            f_copy(s, h, way).wait_recv()
            onward = z + (1 - 2 * way)

            @pl.when((onward >= 0) & (onward < n_z))
            def _():
                f_copy(s, h, way).start()

        @pl.when(t < n_z - 1)
        def _():
            root_send(s, h)

    def first(j, carry):
        @pl.when(j < early)
        def _():
            both(j, arrive)

        @pl.when(j > 0)
        def _():
            both(j - 1, lambda t, h, way, s: finalize(s, 0, h))

        @pl.when(j < early)
        def _():
            both(j, lambda t, h, way, s: partial(s, 0, h))

        return carry

    early = (n_z - 1) * halves
    lax.fori_loop(0, early + 1, first, 0)
    def sel_copy(w, h):
        lane = pl.multiple_of((x if w == 0 else xo) * B + h * H, H)
        return pltpu.make_async_copy(sel_ref.at[:, pl.ds(lane, H)], sel_hbm.at[:, pl.ds(lane, H)], out_s.at[w, h])

    signs = [
        [jnp.where(live(c * out_blocks + b, 2 * p + (x if w == 0 else xo)) > 0, -1.0, 0.0) for b in range(out_blocks)]
        for w in range(2)
    ]

    def write(value, w, h):
        node = x if w == 0 else xo
        lane = pl.multiple_of(node * B + h * H, H)
        for b in range(out_blocks):
            sel_ref[b * B:(b + 1) * B, pl.ds(lane, H)] = (value[b * B:(b + 1) * B] * signs[w][b]).astype(jnp.bfloat16)
        sel_copy(w, h).start()

    def corner(w, r):
        wide = wid_ref[2 * p + w]
        shape = (slice_rows, B)
        line = lax.broadcasted_iota(jnp.int32, shape, 0) + r * slice_rows
        col = lax.broadcasted_iota(jnp.int32, shape, 1)
        own = dinv_ref[r * slice_rows:(r + 1) * slice_rows, w * B:(w + 1) * B]
        return jnp.where((line < wide) & (col < wide), own, 0.0)

    for r in range(n_z):
        for w in range(n_x):
            diag_ref[r * slice_rows:(r + 1) * slice_rows, w * B:(w + 1) * B] = corner(w, r)
    a_copy.wait_recv()

    def second(j, carry):
        @pl.when(j < early)
        def _():
            both(j, lambda t, h, way, s: partial(s, 1, h))

        @pl.when(j > 0)
        def _():
            both(j - 1, lambda t, h, way, s: finalize(s, 1, h))

        return carry

    lax.fori_loop(0, early + 1, second, 0)

    late = n_z - 1 - z
    at_end = (z == 0) | (z == n_z - 1)
    late_owner = at_end & (p == late)
    late_root = at_end & (p == z)

    def late_pair(h):
        return remote(late_out.at[h], late_in.at[h], late_ps.at[h], late_pr.at[h], mate, c)

    def late_copy(h, i, to):
        return remote(late_sum.at[h], late_cin.at[y, core, h], late_ss.at[i, h], late_cr.at[y, core, h], to, c)

    def third_act(t, h, way, s):
        arrive(t, h, way, s)

        def each(i, carry):
            value = jnp.dot(a_buf[jnp.where(i == 0, 1 - core, core)], fbuf[s, h], preferred_element_type=jnp.float32)

            @pl.when(i == 0)
            def _():
                late_out[h] = value.astype(jnp.bfloat16)
                late_pair(h).start()

            @pl.when(i == 1)
            def _():
                late_keep[h] = value

            return carry

        lax.fori_loop(0, 2, each, 0)
        late_pair(h).wait_recv()
        value = (late_keep[h] + late_in[h].astype(jnp.float32)).astype(jnp.bfloat16)
        late_sum[h] = value

        @pl.when((p == z) | (p == late))
        def _():
            late_cin[y, core, h] = value

        @pl.when(p != z)
        def _():
            late_copy(h, 0, z).start()

        @pl.when(p != late)
        def _():
            late_copy(h, 1, late).start()

    def late_total(r, h):
        for g in range(2):
            @pl.when(2 * g + r != p)
            def _():
                remote(
                    late_sum.at[h], late_cin.at[g, r, h], late_ss.at[0, h], late_cr.at[g, r, h], p, c
                ).wait_recv()
        return late_cin[0, r, h].astype(jnp.float32) + late_cin[1, r, h].astype(jnp.float32)

    def third(j, carry):
        both(j, third_act)
        return carry


    def total(r, h):
        part_copy(r, h).wait_recv()
        cross_copy(core, r, h).wait_recv()
        return pown[r, h] + part_in[r, h].astype(jnp.float32) + cross_in[r, h].astype(jnp.float32)

    starts = [pl.multiple_of(x * rows, rows), pl.multiple_of(xo * rows, rows)]

    def d1_copy(to, own, h):
        return remote(
            dpart.at[h, pl.ds(pl.multiple_of(to * slice_rows, slice_rows), slice_rows)], drec.at[own, h],
            d1_s.at[to, h], d1_r.at[own, h], p, to * n_x + x,
        )

    def late_d1(to, h):
        return remote(
            late_dpart.at[h, to * slice_rows:(to + 1) * slice_rows], drec.at[z, h],
            late_ds.at[to, h], d1_r.at[z, h], late, to * n_x + x,
        )

    def diag_half(out, h):
        out[h] = jnp.dot(
            froot_t[...], pall[:, h * H:(h + 1) * H], preferred_element_type=jnp.float32
        ).astype(jnp.bfloat16)

    def late_half(h):
        @pl.when(late_root)
        def _():
            for r in range(2):
                pall[pl.ds(starts[r], rows), h * H:(h + 1) * H] = late_total(r, h).astype(jnp.bfloat16)
            diag_half(late_dpart, h)
            for to in range(n_z):
                late_d1(to, h).start()

    lax.fori_loop(early, early + 1, third, 0)

    @pl.when(jnp.logical_not(late_owner))
    def _():
        for h in range(halves):
            @pl.when(p != z)
            def _():
                root_copy(p, h).wait_recv()
            froot_t[h * H:(h + 1) * H, :] = jnp.transpose(froot[h])
            value = total(1, h).astype(jnp.bfloat16)
            pbf[h] = value
            x_copy(h).start()
            pall[pl.ds(starts[1], rows), h * H:(h + 1) * H] = value
            value = total(0, h)
            pall[pl.ds(starts[0], rows), h * H:(h + 1) * H] = value.astype(jnp.bfloat16)
            write(value, 0, h)
        for h in range(halves):
            diag_half(dpart, h)
            drec[z, h] = dpart[h, pl.ds(pl.multiple_of(z * slice_rows, slice_rows), slice_rows)]
            for d in range(1, n_z):
                d1_copy(lax.rem(z + d, n_z), z, h).start()

    lax.fori_loop(early + 1, early + halves, third, 0)

    @pl.when(late_root)
    def _():
        for h in range(halves):
            froot_t[h * H:(h + 1) * H, :] = jnp.transpose(fbuf[late, h])

    late_half(0)

    @pl.when(late_owner)
    def _():
        for h in range(halves):
            pbf[h] = late_total(1, h).astype(jnp.bfloat16)
            x_copy(h).start()
            write(late_total(0, h), 0, h)

    for h in range(1, halves):
        late_half(h)

    def d2_copy(to, own, h):
        return remote(dall.at[own, h], dall.at[own, h], d2_s.at[to, h], d2_r.at[own, h], p, to)

    for h in range(halves):
        value = jnp.zeros((slice_rows, H), jnp.float32)
        for q in range(n_z):
            @pl.when((q != z) | late_owner)
            def _():
                d1_copy(q, q, h).wait_recv()
            value = value + drec[q, h].astype(jnp.float32)
        dall[c, h] = value.astype(jnp.bfloat16)
        for d in range(1, n_z * n_x):
            d2_copy(lax.rem(c + d, n_z * n_x), c, h).start()

    for h in range(halves):
        x_copy(h).wait_recv()
        write(pnb[h].astype(jnp.float32), 1, h)

    for h in range(halves):
        for d in range(1, n_z * n_x):
            q = lax.rem(c + d, n_z * n_x)
            d2_copy(q, q, h).wait_recv()
    for r in range(n_z):
        for w in range(n_x):
            for h in range(halves):
                diag_ref[r * slice_rows:(r + 1) * slice_rows, w * B + h * H:w * B + (h + 1) * H] += (
                    dall[r * n_x + w, h].astype(jnp.float32)
                )
    diag_copy = pltpu.make_async_copy(diag_ref, diag_hbm, out_s.at[2, 0])
    diag_copy.start()

    a_copy.wait_send()
    for h in range(halves):
        x_copy(h).wait_send()
        @pl.when(at_end)
        def _():
            late_pair(h).wait_send()

            @pl.when(p != z)
            def _():
                late_copy(h, 0, z).wait_send()

            @pl.when(p != late)
            def _():
                late_copy(h, 1, late).wait_send()

    for s in range(n_z):
        off = (s == late) & at_end
        for h in range(halves):
            @pl.when((s <= z) & (z < n_z - 1))
            def _():
                f_copy(s, h, 0).wait_send()

            @pl.when((s >= z) & (z > 0))
            def _():
                f_copy(s, h, 1).wait_send()

            @pl.when((p == z) & (s != z) & jnp.logical_not(off))
            def _():
                root_copy(s, h).wait_send()

            @pl.when(jnp.logical_not(off) & (s == mate))
            def _():
                for r in range(2):
                    part_copy(r, h).wait_send()

            @pl.when(jnp.logical_not(off) & (lax.div(jnp.int32(s), 2) != y))
            def _():
                pair_copy(s % 2, h).wait_send()
                cross_copy(s % 2, core, h).wait_send()

    for h in range(halves):
        @pl.when(jnp.logical_not(late_owner))
        def _():
            for d in range(1, n_z):
                d1_copy(lax.rem(z + d, n_z), z, h).wait_send()

        @pl.when(late_root)
        def _():
            for to in range(n_z):
                late_d1(to, h).wait_send()

        for d in range(1, n_z * n_x):
            d2_copy(lax.rem(c + d, n_z * n_x), c, h).wait_send()
        for w in range(2):
            sel_copy(w, h).wait()
    diag_copy.wait()


def fused(n_prow, n_pcol, ainv, lpanel, dinv, rowblocks, counts, widths):
    n_z, n_x = n_prow, 2
    rows, depth = ainv.shape
    bf, f32, H = jnp.bfloat16, jnp.float32, 128
    halves = B // H
    hbm = pl.BlockSpec(memory_space=pltpu.HBM)
    dma = pltpu.SemaphoreType.DMA
    piece = (2, halves, rows, H)
    results = pl.pallas_call(
        functools.partial(level_kernel, n_z, n_x),
        out_shape=(
            jax.ShapeDtypeStruct((rows, dinv.shape[1]), bf),
            jax.ShapeDtypeStruct(dinv.shape, f32),
        ),
        in_specs=[hbm] * 6,
        out_specs=(hbm, hbm),
        scratch_shapes=[
            pltpu.VMEM((rows, dinv.shape[1]), bf),
            pltpu.VMEM(dinv.shape, f32),
            pltpu.VMEM((2, rows, depth), bf),
            pltpu.VMEM(lpanel.shape, bf),
            pltpu.VMEM(dinv.shape, f32),
            pltpu.SMEM(rowblocks.shape, jnp.int32),
            pltpu.SMEM(counts.shape, jnp.int32),
            pltpu.SMEM(widths.shape, jnp.int32),
            pltpu.VMEM((n_z, halves, depth, H), bf),
            pltpu.VMEM((halves, depth, H), bf),
            pltpu.VMEM((B, depth), bf),
            pltpu.VMEM(piece, f32),
            pltpu.VMEM(piece, f32),
        ]
        + [pltpu.VMEM(piece, bf)] * 6
        + [
            pltpu.VMEM((depth, B), bf),
            pltpu.VMEM((halves, rows, H), bf),
            pltpu.VMEM((halves, rows, H), bf),
            pltpu.VMEM((halves, B, H), bf),
            pltpu.VMEM((n_z, halves, B // n_z, H), bf),
            pltpu.VMEM((n_z * n_x, halves, B // n_z, H), bf),
            pltpu.VMEM((halves, rows, H), f32),
            pltpu.VMEM((halves, rows, H), bf),
            pltpu.VMEM((halves, rows, H), bf),
            pltpu.VMEM((halves, rows, H), bf),
            pltpu.VMEM((2, 2, halves, rows, H), bf),
            pltpu.VMEM((halves, B, H), bf),
            dma((6,)),
            dma((2,)),
            dma((2, n_z, halves)),
            dma((n_z, halves)),
            dma((n_z, halves)),
            dma((halves,)),
        ]
        + [dma((2, halves))] * 6
        + [
            dma((halves,)),
            dma((halves,)),
            dma((n_z, halves)),
            dma((n_z, halves)),
            dma((n_z * n_x, halves)),
            dma((n_z * n_x, halves)),
            dma((halves,)),
            dma((halves,)),
            dma((2, halves)),
            dma((2, 2, halves)),
            dma((n_z, halves)),
            dma((3, halves)),
        ],
        compiler_params=pltpu.CompilerParams(
            collective_id=0, has_side_effects=True, vmem_limit_bytes=60 * 1024 * 1024
        ),
        cost_estimate=pl.CostEstimate(
            flops=2 * rows * depth * SNODES * B, bytes_accessed=4 * 1024 * 1024, transcendentals=0
        ),
    )(ainv, lpanel, dinv, rowblocks, counts, widths)
    anywhere = pl.BlockSpec(memory_space=pl.ANY)
    return pl.pallas_call(
        handoff_kernel,
        out_shape=tuple(jax.ShapeDtypeStruct(r.shape, r.dtype) for r in results),
        in_specs=[anywhere] * 2,
        out_specs=(anywhere, anywhere),
        scratch_shapes=[pltpu.VMEM(r.shape, r.dtype) for r in results]
        + [dma((2 * PIECES,)), dma((2 * PIECES,))],
        compiler_params=pltpu.CompilerParams(vmem_limit_bytes=60 * 1024 * 1024),
    )(*results)


def solution(mesh):
    n_prow, n_pcol = mesh.shape["prow"], mesh.shape["pcol"]

    def step(ainv, lpanel, dinv, rowblocks, counts, widths):
        rows, depth = ainv.shape
        whole = n_prow == 4 and n_pcol == 8 and lpanel.shape[1] == B and dinv.shape[1] == 2 * B
        if whole and depth == 2 * rows and depth == lpanel.shape[0] and rows % B == 0 and B % (16 * n_prow) == 0:
            return fused(n_prow, n_pcol, ainv, lpanel, dinv, rowblocks, counts, widths)
        return per_device(ainv, lpanel, dinv, rowblocks, counts, widths)

    placed = (P("pcol", "prow"), P("prow", "pcol"), P(None, "prow"), P(), P(), P())
    return jax.shard_map(
        step,
        mesh=mesh,
        in_specs=placed,
        out_specs=(P("pcol", "prow"), P(None, "prow")),
        check_vma=False,
    )
```

```python
import functools

import jax
import jax.numpy as jnp
from jax import lax
from jax.experimental import pallas as pl
from jax.experimental.pallas import tpu as pltpu
from jax.sharding import PartitionSpec as P

MESH = pl.DeviceIdType.MESH

B = 256
SNODES = 8


def from_root(value, axis, source):
    kept = jnp.where(lax.axis_index(axis) == source, value, 0).astype(value.dtype)
    return lax.psum(kept, axis)


def block_mask(block_ids, column_ids, rowblocks, counts, widths):
    slot_total = rowblocks.shape[1]
    owner_node = column_ids // B
    within = column_ids % B
    chosen = owner_node[:, None] == jnp.arange(SNODES, dtype=jnp.int32)[None, :]
    owner_rows = jnp.sum(jnp.where(chosen[:, :, None], rowblocks[None, :, :], 0), axis=1)
    owner_count = jnp.sum(jnp.where(chosen, counts[None, :], 0), axis=1)
    owner_width = jnp.sum(jnp.where(chosen, widths[None, :], 0), axis=1)
    slot_live = jnp.arange(slot_total, dtype=jnp.int32)[None, :] < owner_count[:, None]
    matched = (owner_rows[None, :, :] == block_ids[:, None, None]) & slot_live[None, :, :]
    present = jnp.any(matched, axis=2) & (within < owner_width)[None, :]
    return (present, owner_width, within)


def per_device(ainv, lpanel, dinv, rowblocks, counts, widths):
    row_group = lax.axis_index("prow")
    col_group = lax.axis_index("pcol")
    panel_rows = lpanel.shape[0]
    panel_cols = lpanel.shape[1]
    inverse_rows = ainv.shape[0]
    share_cols = dinv.shape[1]
    row_blocks = panel_rows // B
    col_blocks = inverse_rows // B
    own_ids = row_group * row_blocks + jnp.arange(row_blocks, dtype=jnp.int32)
    own_cols = col_group * panel_cols + jnp.arange(panel_cols, dtype=jnp.int32)
    present, unused_width, unused_within = block_mask(own_ids, own_cols, rowblocks, counts, widths)
    masked = jnp.where(
        present[:, None, :], lpanel.reshape(row_blocks, B, panel_cols), jnp.zeros((), jnp.bfloat16)
    )
    masked = masked.reshape(panel_rows, panel_cols)
    gathered = lax.all_gather(masked, "pcol", axis=1, tiled=True)
    product = jnp.dot(ainv, gathered, preferred_element_type=jnp.float32)
    root_row = col_group * col_blocks // row_blocks
    offset = (col_group * col_blocks - root_row * row_blocks) * B
    own_rows = lax.dynamic_slice_in_dim(gathered, offset, inverse_rows, 0)
    width_cols = max(share_cols, B)
    first_col = row_group * share_cols // width_cols * width_cols
    summed = lax.psum_scatter(
        product.astype(jnp.bfloat16), "prow", scatter_dimension=1, tiled=True
    ).astype(jnp.float32)
    whole_rows = from_root(own_rows, "prow", root_row)
    across = lax.dynamic_slice_in_dim(whole_rows, first_col, width_cols, 1)
    column_ids = row_group * share_cols + jnp.arange(share_cols, dtype=jnp.int32)
    block_ids = col_group * col_blocks + jnp.arange(col_blocks, dtype=jnp.int32)
    kept, owner_width, within = block_mask(block_ids, column_ids, rowblocks, counts, widths)
    negated = jnp.where(
        kept[:, None, :], -summed.reshape(col_blocks, B, share_cols), jnp.zeros((), jnp.float32)
    )
    selected_inverse = negated.reshape(inverse_rows, share_cols).astype(jnp.bfloat16)
    groups = max(1, share_cols // B)
    left_side = across.reshape(inverse_rows, groups, width_cols // groups).astype(jnp.float32)
    right_side = summed.reshape(inverse_rows, groups, share_cols // groups)
    quadratic = jnp.einsum(
        "rnb,rnc->bnc", left_side, right_side, precision=lax.Precision.HIGHEST
    ).reshape(B, share_cols)
    quadratic = lax.psum(quadratic.astype(jnp.bfloat16), "pcol").astype(jnp.float32)
    corner = (jnp.arange(B, dtype=jnp.int32)[:, None] < owner_width[None, :]) & (
        within < owner_width
    )[None, :]
    diagonal_blocks = jnp.where(corner, dinv, jnp.zeros((), jnp.float32)) + quadratic
    return (selected_inverse, diagonal_blocks)


PIECES = 2


def handoff_kernel(sel_in, diag_in, sel_out, diag_out, sel_held, diag_held, in_sem, out_sem):
    reads, writes = [], []
    for k, (src, held, dst) in enumerate([(sel_in, sel_held, sel_out), (diag_in, diag_held, diag_out)]):
        part = src.shape[0] // PIECES
        for i in range(PIECES):
            piece = pl.ds(i * part, part)
            n = k * PIECES + i
            reads.append(pltpu.make_async_copy(src.at[piece], held.at[piece], in_sem.at[n]))
            writes.append(pltpu.make_async_copy(held.at[piece], dst.at[piece], out_sem.at[n]))
    for copy in reads:
        copy.start()
    for read, write in zip(reads, writes):
        read.wait()
        write.start()
    for copy in writes:
        copy.wait()


def level_kernel(
    n_z, n_x,
    a_hbm, lp_hbm, dinv_hbm, rb_hbm, cnt_hbm, wid_hbm,
    sel_hbm, diag_hbm,
    sel_ref, diag_ref, a_buf, lp_ref, dinv_ref, rb_ref, cnt_ref, wid_ref,
    fbuf, froot, froot_t, pown, pkeep, pair_out, pair_in, cross_out, cross_in, part_out, part_in,
    pall, pbf, pnb, dpart, drec, dall,
    late_keep, late_out, late_in, late_sum, late_cin, late_dpart,
    in_sem, a_sem, fsend, frecv, rsend, rrecv,
    pair_s, pair_r, cross_s, cross_r, part_s, part_r, xsem_s, xsem_r,
    d1_s, d1_r, d2_s, d2_r, late_ps, late_pr, late_ss, late_cr, late_ds, out_s,
):
    p = lax.axis_index("prow")
    c = lax.axis_index("pcol")
    z = lax.div(c, n_x)
    x = lax.rem(c, n_x)
    xo = 1 - x
    y = lax.div(p, 2)
    core = lax.rem(p, 2)
    mate = 2 * y + 1 - core
    rows = a_hbm.shape[0]
    H = 128
    halves = B // H
    slots = rb_ref.shape[1]
    row_blocks = lp_ref.shape[0] // B
    out_blocks = rows // B
    slice_rows = B // n_z

    fetches = [
        pltpu.make_async_copy(src, dst, in_sem.at[i])
        for i, (src, dst) in enumerate(
            [
                (rb_hbm, rb_ref), (cnt_hbm, cnt_ref), (wid_hbm, wid_ref),
                (lp_hbm, lp_ref), (a_hbm, a_buf.at[0]), (dinv_hbm, dinv_ref),
            ]
        )
    ]
    for fetch in fetches:
        fetch.start()

    def live(block, node):
        count = cnt_ref[node]
        hit = jnp.int32(0)
        for i in range(slots):
            hit += jnp.where((rb_ref[node, i] == block) & (i < count), 1, 0)
        return hit

    def remote(src, dst, s_sem, r_sem, prow, pcol):
        return pltpu.make_async_remote_copy(
            src_ref=src, dst_ref=dst, send_sem=s_sem, recv_sem=r_sem,
            device_id=(prow, pcol), device_id_type=MESH,
        )

    barrier = pltpu.get_barrier_semaphore()
    spot = z * n_z + p
    for d in range(1, n_z * n_z):
        q = lax.rem(spot + d, n_z * n_z)
        pl.semaphore_signal(
            barrier, inc=1, device_id=(lax.rem(q, n_z), lax.div(q, n_z) * n_x + x), device_id_type=MESH
        )
    for d in range(n_z):
        pl.semaphore_signal(barrier, inc=1, device_id=(p, d * n_x + xo), device_id_type=MESH)

    a_copy = remote(a_buf.at[0], a_buf.at[1], a_sem.at[0], a_sem.at[1], p, z * n_x + xo)

    def f_copy(s, h, way):
        return remote(
            fbuf.at[s, h], fbuf.at[s, h], fsend.at[way, s, h], frecv.at[s, h],
            p, (z + (1 - 2 * way)) * n_x + x,
        )

    def root_copy(s, h):
        return remote(fbuf.at[s, h], froot.at[h], rsend.at[s, h], rrecv.at[h], s, c)

    def part_copy(r, h):
        return remote(part_out.at[r, h], part_in.at[r, h], part_s.at[r, h], part_r.at[r, h], mate, c)

    def pair_copy(e, h):
        return remote(pair_out.at[e, h], pair_in.at[e, h], pair_s.at[e, h], pair_r.at[e, h], mate, c)

    def cross_copy(e, r, h):
        return remote(
            cross_out.at[e, h], cross_in.at[r, h], cross_s.at[e, h], cross_r.at[r, h], 2 * (1 - y) + e, c
        )

    def x_copy(h):
        return remote(pbf.at[h], pnb.at[h], xsem_s.at[h], xsem_r.at[h], p, z * n_x + xo)

    def partial(s, r, h):
        value = jnp.dot(a_buf[r], fbuf[s, h], preferred_element_type=jnp.float32)
        e = lax.rem(s, 2)
        same = lax.div(s, 2) == y

        @pl.when(same & (s == p))
        def _():
            pown[r, h] = value

        @pl.when(same & (s != p))
        def _():
            part_out[r, h] = value.astype(jnp.bfloat16)
            part_copy(r, h).start()

        @pl.when(jnp.logical_not(same) & (r == core))
        def _():
            pkeep[e, h] = value

        @pl.when(jnp.logical_not(same) & (r != core))
        def _():
            pair_out[e, h] = value.astype(jnp.bfloat16)
            pair_copy(e, h).start()

    def finalize(s, r, h):
        e = lax.rem(s, 2)

        @pl.when((lax.div(s, 2) != y) & (r == core))
        def _():
            pair_copy(e, h).wait_recv()
            cross_out[e, h] = (pkeep[e, h] + pair_in[e, h].astype(jnp.float32)).astype(jnp.bfloat16)
            cross_copy(e, r, h).start()

    def root_send(s, h):
        @pl.when(p == z)
        def _():
            @pl.when(s != z)
            def _():
                root_copy(s, h).start()

            @pl.when(s == z)
            def _():
                froot[h] = fbuf[s, h]

    for fetch in fetches[:4]:
        fetch.wait()
    width = wid_ref[c]
    limits = [jnp.where(live(p * row_blocks + b, c) > 0, width, 0) for b in range(row_blocks)]
    for h in range(halves):
        for b in range(row_blocks):
            cols = lax.broadcasted_iota(jnp.int32, (B, H), 1) + h * H
            value = lp_ref[b * B:(b + 1) * B, h * H:(h + 1) * H].astype(jnp.float32)
            fbuf[z, h, b * B:(b + 1) * B, :] = jnp.where(cols < limits[b], value, 0.0).astype(jnp.bfloat16)
        if h == 0:
            pl.semaphore_wait(barrier, n_z * n_z - 1 + n_z)

        @pl.when(z < n_z - 1)
        def _():
            f_copy(z, h, 0).start()

        @pl.when(z > 0)
        def _():
            f_copy(z, h, 1).start()

        if h == 0:
            fetches[4].wait()
            a_copy.start()
    fetches[5].wait()

    def both(j, act):
        t = lax.div(j, halves)
        h = lax.rem(j, halves)
        for way in range(2):
            s = z - t * (1 - 2 * way)
            valid = (s >= 0) & (s < n_z)
            if way == 1:
                valid = valid & (t > 0)

            @pl.when(valid)
            def _():
                act(t, h, way, s)

    def arrive(t, h, way, s):
        @pl.when(t > 0)
        def _():
            f_copy(s, h, way).wait_recv()
            onward = z + (1 - 2 * way)

            @pl.when((onward >= 0) & (onward < n_z))
            def _():
                f_copy(s, h, way).start()

        @pl.when(t < n_z - 1)
        def _():
            root_send(s, h)

    def first(j, carry):
        @pl.when(j < early)
        def _():
            both(j, arrive)

        @pl.when(j > 0)
        def _():
            both(j - 1, lambda t, h, way, s: finalize(s, 0, h))

        @pl.when(j < early)
        def _():
            both(j, lambda t, h, way, s: partial(s, 0, h))

        return carry

    early = (n_z - 1) * halves
    lax.fori_loop(0, early + 1, first, 0)
    def sel_copy(w, h):
        lane = pl.multiple_of((x if w == 0 else xo) * B + h * H, H)
        return pltpu.make_async_copy(sel_ref.at[:, pl.ds(lane, H)], sel_hbm.at[:, pl.ds(lane, H)], out_s.at[w, h])

    signs = [
        [jnp.where(live(c * out_blocks + b, 2 * p + (x if w == 0 else xo)) > 0, -1.0, 0.0) for b in range(out_blocks)]
        for w in range(2)
    ]

    def write(value, w, h):
        node = x if w == 0 else xo
        lane = pl.multiple_of(node * B + h * H, H)
        for b in range(out_blocks):
            sel_ref[b * B:(b + 1) * B, pl.ds(lane, H)] = (value[b * B:(b + 1) * B] * signs[w][b]).astype(jnp.bfloat16)
        sel_copy(w, h).start()

    def corner(w, r):
        wide = wid_ref[2 * p + w]
        shape = (slice_rows, B)
        line = lax.broadcasted_iota(jnp.int32, shape, 0) + r * slice_rows
        col = lax.broadcasted_iota(jnp.int32, shape, 1)
        own = dinv_ref[r * slice_rows:(r + 1) * slice_rows, w * B:(w + 1) * B]
        return jnp.where((line < wide) & (col < wide), own, 0.0)

    for r in range(n_z):
        for w in range(n_x):
            diag_ref[r * slice_rows:(r + 1) * slice_rows, w * B:(w + 1) * B] = corner(w, r)
    a_copy.wait_recv()

    def second(j, carry):
        @pl.when(j < early)
        def _():
            both(j, lambda t, h, way, s: partial(s, 1, h))

        @pl.when(j > 0)
        def _():
            both(j - 1, lambda t, h, way, s: finalize(s, 1, h))

        return carry

    lax.fori_loop(0, early + 1, second, 0)

    late = n_z - 1 - z
    at_end = (z == 0) | (z == n_z - 1)
    late_owner = at_end & (p == late)
    late_root = at_end & (p == z)

    def late_pair(h):
        return remote(late_out.at[h], late_in.at[h], late_ps.at[h], late_pr.at[h], mate, c)

    def late_copy(h, i, to):
        return remote(late_sum.at[h], late_cin.at[y, core, h], late_ss.at[i, h], late_cr.at[y, core, h], to, c)

    def third_act(t, h, way, s):
        arrive(t, h, way, s)

        def each(i, carry):
            value = jnp.dot(a_buf[jnp.where(i == 0, 1 - core, core)], fbuf[s, h], preferred_element_type=jnp.float32)

            @pl.when(i == 0)
            def _():
                late_out[h] = value.astype(jnp.bfloat16)
                late_pair(h).start()

            @pl.when(i == 1)
            def _():
                late_keep[h] = value

            return carry

        lax.fori_loop(0, 2, each, 0)
        late_pair(h).wait_recv()
        value = (late_keep[h] + late_in[h].astype(jnp.float32)).astype(jnp.bfloat16)
        late_sum[h] = value

        @pl.when((p == z) | (p == late))
        def _():
            late_cin[y, core, h] = value

        @pl.when(p != z)
        def _():
            late_copy(h, 0, z).start()

        @pl.when(p != late)
        def _():
            late_copy(h, 1, late).start()

    def late_total(r, h):
        for g in range(2):
            @pl.when(2 * g + r != p)
            def _():
                remote(
                    late_sum.at[h], late_cin.at[g, r, h], late_ss.at[0, h], late_cr.at[g, r, h], p, c
                ).wait_recv()
        return late_cin[0, r, h].astype(jnp.float32) + late_cin[1, r, h].astype(jnp.float32)

    def third(j, carry):
        both(j, third_act)
        return carry

    lax.fori_loop(early, early + halves, third, 0)

    def total(r, h):
        part_copy(r, h).wait_recv()
        cross_copy(core, r, h).wait_recv()
        return pown[r, h] + part_in[r, h].astype(jnp.float32) + cross_in[r, h].astype(jnp.float32)

    starts = [pl.multiple_of(x * rows, rows), pl.multiple_of(xo * rows, rows)]

    def d1_copy(to, own, h):
        return remote(
            dpart.at[h, pl.ds(pl.multiple_of(to * slice_rows, slice_rows), slice_rows)], drec.at[own, h],
            d1_s.at[to, h], d1_r.at[own, h], p, to * n_x + x,
        )

    def late_d1(to, h):
        return remote(
            late_dpart.at[h, to * slice_rows:(to + 1) * slice_rows], drec.at[z, h],
            late_ds.at[to, h], d1_r.at[z, h], late, to * n_x + x,
        )

    def diag_half(out, h):
        out[h] = jnp.dot(
            froot_t[...], pall[:, h * H:(h + 1) * H], preferred_element_type=jnp.float32
        ).astype(jnp.bfloat16)

    def late_half(h):
        @pl.when(late_root)
        def _():
            for r in range(2):
                pall[pl.ds(starts[r], rows), h * H:(h + 1) * H] = late_total(r, h).astype(jnp.bfloat16)
            diag_half(late_dpart, h)
            for to in range(n_z):
                late_d1(to, h).start()

    @pl.when(late_root)
    def _():
        for h in range(halves):
            froot_t[h * H:(h + 1) * H, :] = jnp.transpose(fbuf[late, h])

    late_half(0)

    @pl.when(jnp.logical_not(late_owner))
    def _():
        for h in range(halves):
            @pl.when(p != z)
            def _():
                root_copy(p, h).wait_recv()
            froot_t[h * H:(h + 1) * H, :] = jnp.transpose(froot[h])
            value = total(1, h).astype(jnp.bfloat16)
            pbf[h] = value
            x_copy(h).start()
            pall[pl.ds(starts[1], rows), h * H:(h + 1) * H] = value
            value = total(0, h)
            pall[pl.ds(starts[0], rows), h * H:(h + 1) * H] = value.astype(jnp.bfloat16)
            write(value, 0, h)
        for h in range(halves):
            diag_half(dpart, h)
            drec[z, h] = dpart[h, pl.ds(pl.multiple_of(z * slice_rows, slice_rows), slice_rows)]
            for d in range(1, n_z):
                d1_copy(lax.rem(z + d, n_z), z, h).start()

    @pl.when(late_owner)
    def _():
        for h in range(halves):
            pbf[h] = late_total(1, h).astype(jnp.bfloat16)
            x_copy(h).start()
            write(late_total(0, h), 0, h)

    @pl.when(late_root)
    def _():
        for h in range(halves):
            froot_t[h * H:(h + 1) * H, :] = jnp.transpose(fbuf[late, h])

    for h in range(1, halves):
        late_half(h)

    def d2_copy(to, own, h):
        return remote(dall.at[own, h], dall.at[own, h], d2_s.at[to, h], d2_r.at[own, h], p, to)

    for h in range(halves):
        value = jnp.zeros((slice_rows, H), jnp.float32)
        for q in range(n_z):
            @pl.when((q != z) | late_owner)
            def _():
                d1_copy(q, q, h).wait_recv()
            value = value + drec[q, h].astype(jnp.float32)
        dall[c, h] = value.astype(jnp.bfloat16)
        for d in range(1, n_z * n_x):
            d2_copy(lax.rem(c + d, n_z * n_x), c, h).start()

    for h in range(halves):
        x_copy(h).wait_recv()
        write(pnb[h].astype(jnp.float32), 1, h)

    for h in range(halves):
        for d in range(1, n_z * n_x):
            q = lax.rem(c + d, n_z * n_x)
            d2_copy(q, q, h).wait_recv()
    for r in range(n_z):
        for w in range(n_x):
            for h in range(halves):
                diag_ref[r * slice_rows:(r + 1) * slice_rows, w * B + h * H:w * B + (h + 1) * H] += (
                    dall[r * n_x + w, h].astype(jnp.float32)
                )
    diag_copy = pltpu.make_async_copy(diag_ref, diag_hbm, out_s.at[2, 0])
    diag_copy.start()

    a_copy.wait_send()
    for h in range(halves):
        x_copy(h).wait_send()
        @pl.when(at_end)
        def _():
            late_pair(h).wait_send()

            @pl.when(p != z)
            def _():
                late_copy(h, 0, z).wait_send()

            @pl.when(p != late)
            def _():
                late_copy(h, 1, late).wait_send()

    for s in range(n_z):
        off = (s == late) & at_end
        for h in range(halves):
            @pl.when((s <= z) & (z < n_z - 1))
            def _():
                f_copy(s, h, 0).wait_send()

            @pl.when((s >= z) & (z > 0))
            def _():
                f_copy(s, h, 1).wait_send()

            @pl.when((p == z) & (s != z) & jnp.logical_not(off))
            def _():
                root_copy(s, h).wait_send()

            @pl.when(jnp.logical_not(off) & (s == mate))
            def _():
                for r in range(2):
                    part_copy(r, h).wait_send()

            @pl.when(jnp.logical_not(off) & (lax.div(jnp.int32(s), 2) != y))
            def _():
                pair_copy(s % 2, h).wait_send()
                cross_copy(s % 2, core, h).wait_send()

    for h in range(halves):
        @pl.when(jnp.logical_not(late_owner))
        def _():
            for d in range(1, n_z):
                d1_copy(lax.rem(z + d, n_z), z, h).wait_send()

        @pl.when(late_root)
        def _():
            for to in range(n_z):
                late_d1(to, h).wait_send()

        for d in range(1, n_z * n_x):
            d2_copy(lax.rem(c + d, n_z * n_x), c, h).wait_send()
        for w in range(2):
            sel_copy(w, h).wait()
    diag_copy.wait()


def fused(n_prow, n_pcol, ainv, lpanel, dinv, rowblocks, counts, widths):
    n_z, n_x = n_prow, 2
    rows, depth = ainv.shape
    bf, f32, H = jnp.bfloat16, jnp.float32, 128
    halves = B // H
    hbm = pl.BlockSpec(memory_space=pltpu.HBM)
    dma = pltpu.SemaphoreType.DMA
    piece = (2, halves, rows, H)
    results = pl.pallas_call(
        functools.partial(level_kernel, n_z, n_x),
        out_shape=(
            jax.ShapeDtypeStruct((rows, dinv.shape[1]), bf),
            jax.ShapeDtypeStruct(dinv.shape, f32),
        ),
        in_specs=[hbm] * 6,
        out_specs=(hbm, hbm),
        scratch_shapes=[
            pltpu.VMEM((rows, dinv.shape[1]), bf),
            pltpu.VMEM(dinv.shape, f32),
            pltpu.VMEM((2, rows, depth), bf),
            pltpu.VMEM(lpanel.shape, bf),
            pltpu.VMEM(dinv.shape, f32),
            pltpu.SMEM(rowblocks.shape, jnp.int32),
            pltpu.SMEM(counts.shape, jnp.int32),
            pltpu.SMEM(widths.shape, jnp.int32),
            pltpu.VMEM((n_z, halves, depth, H), bf),
            pltpu.VMEM((halves, depth, H), bf),
            pltpu.VMEM((B, depth), bf),
            pltpu.VMEM(piece, f32),
            pltpu.VMEM(piece, f32),
        ]
        + [pltpu.VMEM(piece, bf)] * 6
        + [
            pltpu.VMEM((depth, B), bf),
            pltpu.VMEM((halves, rows, H), bf),
            pltpu.VMEM((halves, rows, H), bf),
            pltpu.VMEM((halves, B, H), bf),
            pltpu.VMEM((n_z, halves, B // n_z, H), bf),
            pltpu.VMEM((n_z * n_x, halves, B // n_z, H), bf),
            pltpu.VMEM((halves, rows, H), f32),
            pltpu.VMEM((halves, rows, H), bf),
            pltpu.VMEM((halves, rows, H), bf),
            pltpu.VMEM((halves, rows, H), bf),
            pltpu.VMEM((2, 2, halves, rows, H), bf),
            pltpu.VMEM((halves, B, H), bf),
            dma((6,)),
            dma((2,)),
            dma((2, n_z, halves)),
            dma((n_z, halves)),
            dma((n_z, halves)),
            dma((halves,)),
        ]
        + [dma((2, halves))] * 6
        + [
            dma((halves,)),
            dma((halves,)),
            dma((n_z, halves)),
            dma((n_z, halves)),
            dma((n_z * n_x, halves)),
            dma((n_z * n_x, halves)),
            dma((halves,)),
            dma((halves,)),
            dma((2, halves)),
            dma((2, 2, halves)),
            dma((n_z, halves)),
            dma((3, halves)),
        ],
        compiler_params=pltpu.CompilerParams(
            collective_id=0, has_side_effects=True, vmem_limit_bytes=60 * 1024 * 1024
        ),
        cost_estimate=pl.CostEstimate(
            flops=2 * rows * depth * SNODES * B, bytes_accessed=4 * 1024 * 1024, transcendentals=0
        ),
    )(ainv, lpanel, dinv, rowblocks, counts, widths)
    anywhere = pl.BlockSpec(memory_space=pl.ANY)
    return pl.pallas_call(
        handoff_kernel,
        out_shape=tuple(jax.ShapeDtypeStruct(r.shape, r.dtype) for r in results),
        in_specs=[anywhere] * 2,
        out_specs=(anywhere, anywhere),
        scratch_shapes=[pltpu.VMEM(r.shape, r.dtype) for r in results]
        + [dma((2 * PIECES,)), dma((2 * PIECES,))],
        compiler_params=pltpu.CompilerParams(vmem_limit_bytes=60 * 1024 * 1024),
    )(*results)


def solution(mesh):
    n_prow, n_pcol = mesh.shape["prow"], mesh.shape["pcol"]

    def step(ainv, lpanel, dinv, rowblocks, counts, widths):
        rows, depth = ainv.shape
        whole = n_prow == 4 and n_pcol == 8 and lpanel.shape[1] == B and dinv.shape[1] == 2 * B
        if whole and depth == 2 * rows and depth == lpanel.shape[0] and rows % B == 0 and B % (16 * n_prow) == 0:
            return fused(n_prow, n_pcol, ainv, lpanel, dinv, rowblocks, counts, widths)
        return per_device(ainv, lpanel, dinv, rowblocks, counts, widths)

    placed = (P("pcol", "prow"), P("prow", "pcol"), P(None, "prow"), P(), P(), P())
    return jax.shard_map(
        step,
        mesh=mesh,
        in_specs=placed,
        out_specs=(P("pcol", "prow"), P(None, "prow")),
        check_vma=False,
    )
```

```python
import functools

import jax
import jax.numpy as jnp
from jax import lax
from jax.experimental import pallas as pl
from jax.experimental.pallas import tpu as pltpu
from jax.sharding import PartitionSpec as P

MESH = pl.DeviceIdType.MESH

B = 256
SNODES = 8


def from_root(value, axis, source):
    kept = jnp.where(lax.axis_index(axis) == source, value, 0).astype(value.dtype)
    return lax.psum(kept, axis)


def block_mask(block_ids, column_ids, rowblocks, counts, widths):
    slot_total = rowblocks.shape[1]
    owner_node = column_ids // B
    within = column_ids % B
    chosen = owner_node[:, None] == jnp.arange(SNODES, dtype=jnp.int32)[None, :]
    owner_rows = jnp.sum(jnp.where(chosen[:, :, None], rowblocks[None, :, :], 0), axis=1)
    owner_count = jnp.sum(jnp.where(chosen, counts[None, :], 0), axis=1)
    owner_width = jnp.sum(jnp.where(chosen, widths[None, :], 0), axis=1)
    slot_live = jnp.arange(slot_total, dtype=jnp.int32)[None, :] < owner_count[:, None]
    matched = (owner_rows[None, :, :] == block_ids[:, None, None]) & slot_live[None, :, :]
    present = jnp.any(matched, axis=2) & (within < owner_width)[None, :]
    return (present, owner_width, within)


def per_device(ainv, lpanel, dinv, rowblocks, counts, widths):
    row_group = lax.axis_index("prow")
    col_group = lax.axis_index("pcol")
    panel_rows = lpanel.shape[0]
    panel_cols = lpanel.shape[1]
    inverse_rows = ainv.shape[0]
    share_cols = dinv.shape[1]
    row_blocks = panel_rows // B
    col_blocks = inverse_rows // B
    own_ids = row_group * row_blocks + jnp.arange(row_blocks, dtype=jnp.int32)
    own_cols = col_group * panel_cols + jnp.arange(panel_cols, dtype=jnp.int32)
    present, unused_width, unused_within = block_mask(own_ids, own_cols, rowblocks, counts, widths)
    masked = jnp.where(
        present[:, None, :], lpanel.reshape(row_blocks, B, panel_cols), jnp.zeros((), jnp.bfloat16)
    )
    masked = masked.reshape(panel_rows, panel_cols)
    gathered = lax.all_gather(masked, "pcol", axis=1, tiled=True)
    product = jnp.dot(ainv, gathered, preferred_element_type=jnp.float32)
    root_row = col_group * col_blocks // row_blocks
    offset = (col_group * col_blocks - root_row * row_blocks) * B
    own_rows = lax.dynamic_slice_in_dim(gathered, offset, inverse_rows, 0)
    width_cols = max(share_cols, B)
    first_col = row_group * share_cols // width_cols * width_cols
    summed = lax.psum_scatter(
        product.astype(jnp.bfloat16), "prow", scatter_dimension=1, tiled=True
    ).astype(jnp.float32)
    whole_rows = from_root(own_rows, "prow", root_row)
    across = lax.dynamic_slice_in_dim(whole_rows, first_col, width_cols, 1)
    column_ids = row_group * share_cols + jnp.arange(share_cols, dtype=jnp.int32)
    block_ids = col_group * col_blocks + jnp.arange(col_blocks, dtype=jnp.int32)
    kept, owner_width, within = block_mask(block_ids, column_ids, rowblocks, counts, widths)
    negated = jnp.where(
        kept[:, None, :], -summed.reshape(col_blocks, B, share_cols), jnp.zeros((), jnp.float32)
    )
    selected_inverse = negated.reshape(inverse_rows, share_cols).astype(jnp.bfloat16)
    groups = max(1, share_cols // B)
    left_side = across.reshape(inverse_rows, groups, width_cols // groups).astype(jnp.float32)
    right_side = summed.reshape(inverse_rows, groups, share_cols // groups)
    quadratic = jnp.einsum(
        "rnb,rnc->bnc", left_side, right_side, precision=lax.Precision.HIGHEST
    ).reshape(B, share_cols)
    quadratic = lax.psum(quadratic.astype(jnp.bfloat16), "pcol").astype(jnp.float32)
    corner = (jnp.arange(B, dtype=jnp.int32)[:, None] < owner_width[None, :]) & (
        within < owner_width
    )[None, :]
    diagonal_blocks = jnp.where(corner, dinv, jnp.zeros((), jnp.float32)) + quadratic
    return (selected_inverse, diagonal_blocks)


PIECES = 2


def handoff_kernel(sel_in, diag_in, sel_out, diag_out, sel_held, diag_held, in_sem, out_sem):
    reads, writes = [], []
    for k, (src, held, dst) in enumerate([(sel_in, sel_held, sel_out), (diag_in, diag_held, diag_out)]):
        part = src.shape[0] // PIECES
        for i in range(PIECES):
            piece = pl.ds(i * part, part)
            n = k * PIECES + i
            reads.append(pltpu.make_async_copy(src.at[piece], held.at[piece], in_sem.at[n]))
            writes.append(pltpu.make_async_copy(held.at[piece], dst.at[piece], out_sem.at[n]))
    for copy in reads:
        copy.start()
    for read, write in zip(reads, writes):
        read.wait()
        write.start()
    for copy in writes:
        copy.wait()


def level_kernel(
    n_z, n_x,
    a_hbm, lp_hbm, dinv_hbm, rb_hbm, cnt_hbm, wid_hbm,
    sel_hbm, diag_hbm,
    sel_ref, diag_ref, a_buf, lp_ref, dinv_ref, rb_ref, cnt_ref, wid_ref,
    fbuf, froot, froot_t, pown, pkeep, pair_out, pair_in, cross_out, cross_in, part_out, part_in,
    pall, pbf, pnb, dpart, drec, dall,
    late_keep, late_out, late_in, late_sum, late_cin, late_dpart,
    in_sem, a_sem, fsend, frecv, rsend, rrecv,
    pair_s, pair_r, cross_s, cross_r, part_s, part_r, xsem_s, xsem_r,
    d1_s, d1_r, d2_s, d2_r, late_ps, late_pr, late_ss, late_cr, late_ds, out_s,
):
    p = lax.axis_index("prow")
    c = lax.axis_index("pcol")
    z = lax.div(c, n_x)
    x = lax.rem(c, n_x)
    xo = 1 - x
    y = lax.div(p, 2)
    core = lax.rem(p, 2)
    mate = 2 * y + 1 - core
    rows = a_hbm.shape[0]
    H = 128
    halves = B // H
    slots = rb_ref.shape[1]
    row_blocks = lp_ref.shape[0] // B
    out_blocks = rows // B
    slice_rows = B // n_z

    fetches = [
        pltpu.make_async_copy(src, dst, in_sem.at[i])
        for i, (src, dst) in enumerate(
            [
                (rb_hbm, rb_ref), (cnt_hbm, cnt_ref), (wid_hbm, wid_ref),
                (lp_hbm, lp_ref), (a_hbm, a_buf.at[0]), (dinv_hbm, dinv_ref),
            ]
        )
    ]
    for fetch in fetches:
        fetch.start()

    def live(block, node):
        count = cnt_ref[node]
        hit = jnp.int32(0)
        for i in range(slots):
            hit += jnp.where((rb_ref[node, i] == block) & (i < count), 1, 0)
        return hit

    def remote(src, dst, s_sem, r_sem, prow, pcol):
        return pltpu.make_async_remote_copy(
            src_ref=src, dst_ref=dst, send_sem=s_sem, recv_sem=r_sem,
            device_id=(prow, pcol), device_id_type=MESH,
        )

    barrier = pltpu.get_barrier_semaphore()
    spot = z * n_z + p
    for d in range(1, n_z * n_z):
        q = lax.rem(spot + d, n_z * n_z)
        pl.semaphore_signal(
            barrier, inc=1, device_id=(lax.rem(q, n_z), lax.div(q, n_z) * n_x + x), device_id_type=MESH
        )
    for d in range(n_z):
        pl.semaphore_signal(barrier, inc=1, device_id=(p, d * n_x + xo), device_id_type=MESH)

    a_copy = remote(a_hbm, a_buf.at[1], a_sem.at[0], a_sem.at[1], p, z * n_x + xo)

    def f_copy(s, h, way):
        return remote(
            fbuf.at[s, h], fbuf.at[s, h], fsend.at[way, s, h], frecv.at[s, h],
            p, (z + (1 - 2 * way)) * n_x + x,
        )

    def root_copy(s, h):
        return remote(fbuf.at[s, h], froot.at[h], rsend.at[s, h], rrecv.at[h], s, c)

    def part_copy(r, h):
        return remote(part_out.at[r, h], part_in.at[r, h], part_s.at[r, h], part_r.at[r, h], mate, c)

    def pair_copy(e, h):
        return remote(pair_out.at[e, h], pair_in.at[e, h], pair_s.at[e, h], pair_r.at[e, h], mate, c)

    def cross_copy(e, r, h):
        return remote(
            cross_out.at[e, h], cross_in.at[r, h], cross_s.at[e, h], cross_r.at[r, h], 2 * (1 - y) + e, c
        )

    def x_copy(h):
        return remote(pbf.at[h], pnb.at[h], xsem_s.at[h], xsem_r.at[h], p, z * n_x + xo)

    def partial(s, r, h):
        value = jnp.dot(a_buf[r], fbuf[s, h], preferred_element_type=jnp.float32)
        e = lax.rem(s, 2)
        same = lax.div(s, 2) == y

        @pl.when(same & (s == p))
        def _():
            pown[r, h] = value

        @pl.when(same & (s != p))
        def _():
            part_out[r, h] = value.astype(jnp.bfloat16)
            part_copy(r, h).start()

        @pl.when(jnp.logical_not(same) & (r == core))
        def _():
            pkeep[e, h] = value

        @pl.when(jnp.logical_not(same) & (r != core))
        def _():
            pair_out[e, h] = value.astype(jnp.bfloat16)
            pair_copy(e, h).start()

    def finalize(s, r, h):
        e = lax.rem(s, 2)

        @pl.when((lax.div(s, 2) != y) & (r == core))
        def _():
            pair_copy(e, h).wait_recv()
            cross_out[e, h] = (pkeep[e, h] + pair_in[e, h].astype(jnp.float32)).astype(jnp.bfloat16)
            cross_copy(e, r, h).start()

    def root_send(s, h):
        @pl.when(p == z)
        def _():
            @pl.when(s != z)
            def _():
                root_copy(s, h).start()

            @pl.when(s == z)
            def _():
                froot[h] = fbuf[s, h]

    def own_send(h):
        @pl.when(z < n_z - 1)
        def _():
            f_copy(z, h, 0).start()

        @pl.when(z > 0)
        def _():
            f_copy(z, h, 1).start()

    for fetch in fetches[:4]:
        fetch.wait()
    width = wid_ref[c]
    limits = [jnp.where(live(p * row_blocks + b, c) > 0, width, 0) for b in range(row_blocks)]
    for h in range(halves):
        for b in range(row_blocks):
            cols = lax.broadcasted_iota(jnp.int32, (B, H), 1) + h * H
            value = lp_ref[b * B:(b + 1) * B, h * H:(h + 1) * H].astype(jnp.float32)
            fbuf[z, h, b * B:(b + 1) * B, :] = jnp.where(cols < limits[b], value, 0.0).astype(jnp.bfloat16)
        if h == 0:
            pl.semaphore_wait(barrier, n_z * n_z - 1 + n_z)
            own_send(0)
            a_copy.start()
    for fetch in fetches[4:]:
        fetch.wait()

    def both(j, act):
        t = lax.div(j, halves)
        h = lax.rem(j, halves)
        for way in range(2):
            s = z - t * (1 - 2 * way)
            valid = (s >= 0) & (s < n_z)
            if way == 1:
                valid = valid & (t > 0)

            @pl.when(valid)
            def _():
                act(t, h, way, s)

    def arrive(t, h, way, s):
        @pl.when(t > 0)
        def _():
            f_copy(s, h, way).wait_recv()
            onward = z + (1 - 2 * way)

            @pl.when((onward >= 0) & (onward < n_z))
            def _():
                f_copy(s, h, way).start()

        @pl.when(t < n_z - 1)
        def _():
            root_send(s, h)

    def first(j, carry):
        @pl.when(j < early)
        def _():
            both(j, arrive)

        @pl.when(j > 0)
        def _():
            both(j - 1, lambda t, h, way, s: finalize(s, 0, h))

        @pl.when(j < early)
        def _():
            both(j, lambda t, h, way, s: partial(s, 0, h))

        @pl.when(j < halves - 1)
        def _():
            own_send(j + 1)

        return carry

    early = (n_z - 1) * halves
    lax.fori_loop(0, early + 1, first, 0)
    def sel_copy(w, h):
        lane = pl.multiple_of((x if w == 0 else xo) * B + h * H, H)
        return pltpu.make_async_copy(sel_ref.at[:, pl.ds(lane, H)], sel_hbm.at[:, pl.ds(lane, H)], out_s.at[w, h])

    signs = [
        [jnp.where(live(c * out_blocks + b, 2 * p + (x if w == 0 else xo)) > 0, -1.0, 0.0) for b in range(out_blocks)]
        for w in range(2)
    ]

    def write(value, w, h):
        node = x if w == 0 else xo
        lane = pl.multiple_of(node * B + h * H, H)
        for b in range(out_blocks):
            sel_ref[b * B:(b + 1) * B, pl.ds(lane, H)] = (value[b * B:(b + 1) * B] * signs[w][b]).astype(jnp.bfloat16)
        sel_copy(w, h).start()

    def corner(w, r):
        wide = wid_ref[2 * p + w]
        shape = (slice_rows, B)
        line = lax.broadcasted_iota(jnp.int32, shape, 0) + r * slice_rows
        col = lax.broadcasted_iota(jnp.int32, shape, 1)
        own = dinv_ref[r * slice_rows:(r + 1) * slice_rows, w * B:(w + 1) * B]
        return jnp.where((line < wide) & (col < wide), own, 0.0)

    for r in range(n_z):
        for w in range(n_x):
            diag_ref[r * slice_rows:(r + 1) * slice_rows, w * B:(w + 1) * B] = corner(w, r)
    a_copy.wait_recv()

    def second(j, carry):
        @pl.when(j < early)
        def _():
            both(j, lambda t, h, way, s: partial(s, 1, h))

        @pl.when(j > 0)
        def _():
            both(j - 1, lambda t, h, way, s: finalize(s, 1, h))

        return carry

    lax.fori_loop(0, early + 1, second, 0)

    late = n_z - 1 - z
    at_end = (z == 0) | (z == n_z - 1)
    late_owner = at_end & (p == late)
    late_root = at_end & (p == z)

    def late_pair(h):
        return remote(late_out.at[h], late_in.at[h], late_ps.at[h], late_pr.at[h], mate, c)

    def late_copy(h, i, to):
        return remote(late_sum.at[h], late_cin.at[y, core, h], late_ss.at[i, h], late_cr.at[y, core, h], to, c)

    def third_act(t, h, way, s):
        arrive(t, h, way, s)

        def each(i, carry):
            value = jnp.dot(a_buf[jnp.where(i == 0, 1 - core, core)], fbuf[s, h], preferred_element_type=jnp.float32)

            @pl.when(i == 0)
            def _():
                late_out[h] = value.astype(jnp.bfloat16)
                late_pair(h).start()

            @pl.when(i == 1)
            def _():
                late_keep[h] = value

            return carry

        lax.fori_loop(0, 2, each, 0)
        late_pair(h).wait_recv()
        value = (late_keep[h] + late_in[h].astype(jnp.float32)).astype(jnp.bfloat16)
        late_sum[h] = value

        @pl.when((p == z) | (p == late))
        def _():
            late_cin[y, core, h] = value

        @pl.when(p != z)
        def _():
            late_copy(h, 0, z).start()

        @pl.when(p != late)
        def _():
            late_copy(h, 1, late).start()

    def late_total(r, h):
        for g in range(2):
            @pl.when(2 * g + r != p)
            def _():
                remote(
                    late_sum.at[h], late_cin.at[g, r, h], late_ss.at[0, h], late_cr.at[g, r, h], p, c
                ).wait_recv()
        return late_cin[0, r, h].astype(jnp.float32) + late_cin[1, r, h].astype(jnp.float32)

    def third(j, carry):
        both(j, third_act)
        return carry

    lax.fori_loop(early, early + halves, third, 0)

    def total(r, h):
        part_copy(r, h).wait_recv()
        cross_copy(core, r, h).wait_recv()
        return pown[r, h] + part_in[r, h].astype(jnp.float32) + cross_in[r, h].astype(jnp.float32)

    starts = [pl.multiple_of(x * rows, rows), pl.multiple_of(xo * rows, rows)]

    def d1_copy(to, own, h):
        return remote(
            dpart.at[h, pl.ds(pl.multiple_of(to * slice_rows, slice_rows), slice_rows)], drec.at[own, h],
            d1_s.at[to, h], d1_r.at[own, h], p, to * n_x + x,
        )

    def late_d1(to, h):
        return remote(
            late_dpart.at[h, to * slice_rows:(to + 1) * slice_rows], drec.at[z, h],
            late_ds.at[to, h], d1_r.at[z, h], late, to * n_x + x,
        )

    def diag_half(out, h):
        out[h] = jnp.dot(
            froot_t[...], pall[:, h * H:(h + 1) * H], preferred_element_type=jnp.float32
        ).astype(jnp.bfloat16)

    def late_half(h):
        @pl.when(late_root)
        def _():
            for r in range(2):
                pall[pl.ds(starts[r], rows), h * H:(h + 1) * H] = late_total(r, h).astype(jnp.bfloat16)
            diag_half(late_dpart, h)
            for to in range(n_z):
                late_d1(to, h).start()

    @pl.when(late_root)
    def _():
        for h in range(halves):
            froot_t[h * H:(h + 1) * H, :] = jnp.transpose(fbuf[late, h])

    late_half(0)

    @pl.when(jnp.logical_not(late_owner))
    def _():
        for h in range(halves):
            @pl.when(p != z)
            def _():
                root_copy(p, h).wait_recv()
            froot_t[h * H:(h + 1) * H, :] = jnp.transpose(froot[h])
            value = total(1, h).astype(jnp.bfloat16)
            pbf[h] = value
            x_copy(h).start()
            pall[pl.ds(starts[1], rows), h * H:(h + 1) * H] = value
            value = total(0, h)
            pall[pl.ds(starts[0], rows), h * H:(h + 1) * H] = value.astype(jnp.bfloat16)
            write(value, 0, h)
        for h in range(halves):
            diag_half(dpart, h)
            drec[z, h] = dpart[h, pl.ds(pl.multiple_of(z * slice_rows, slice_rows), slice_rows)]
            for d in range(1, n_z):
                d1_copy(lax.rem(z + d, n_z), z, h).start()

    @pl.when(late_owner)
    def _():
        for h in range(halves):
            pbf[h] = late_total(1, h).astype(jnp.bfloat16)
            x_copy(h).start()
            write(late_total(0, h), 0, h)

    @pl.when(late_root)
    def _():
        for h in range(halves):
            froot_t[h * H:(h + 1) * H, :] = jnp.transpose(fbuf[late, h])

    for h in range(1, halves):
        late_half(h)

    def d2_copy(to, own, h):
        return remote(dall.at[own, h], dall.at[own, h], d2_s.at[to, h], d2_r.at[own, h], p, to)

    for h in range(halves):
        value = jnp.zeros((slice_rows, H), jnp.float32)
        for q in range(n_z):
            @pl.when((q != z) | late_owner)
            def _():
                d1_copy(q, q, h).wait_recv()
            value = value + drec[q, h].astype(jnp.float32)
        dall[c, h] = value.astype(jnp.bfloat16)
        for d in range(1, n_z * n_x):
            d2_copy(lax.rem(c + d, n_z * n_x), c, h).start()

    for h in range(halves):
        x_copy(h).wait_recv()
        write(pnb[h].astype(jnp.float32), 1, h)

    for h in range(halves):
        for d in range(1, n_z * n_x):
            q = lax.rem(c + d, n_z * n_x)
            d2_copy(q, q, h).wait_recv()
    for r in range(n_z):
        for w in range(n_x):
            for h in range(halves):
                diag_ref[r * slice_rows:(r + 1) * slice_rows, w * B + h * H:w * B + (h + 1) * H] += (
                    dall[r * n_x + w, h].astype(jnp.float32)
                )
    diag_copy = pltpu.make_async_copy(diag_ref, diag_hbm, out_s.at[2, 0])
    diag_copy.start()

    a_copy.wait_send()
    for h in range(halves):
        x_copy(h).wait_send()
        @pl.when(at_end)
        def _():
            late_pair(h).wait_send()

            @pl.when(p != z)
            def _():
                late_copy(h, 0, z).wait_send()

            @pl.when(p != late)
            def _():
                late_copy(h, 1, late).wait_send()

    for s in range(n_z):
        off = (s == late) & at_end
        for h in range(halves):
            @pl.when((s <= z) & (z < n_z - 1))
            def _():
                f_copy(s, h, 0).wait_send()

            @pl.when((s >= z) & (z > 0))
            def _():
                f_copy(s, h, 1).wait_send()

            @pl.when((p == z) & (s != z) & jnp.logical_not(off))
            def _():
                root_copy(s, h).wait_send()

            @pl.when(jnp.logical_not(off) & (s == mate))
            def _():
                for r in range(2):
                    part_copy(r, h).wait_send()

            @pl.when(jnp.logical_not(off) & (lax.div(jnp.int32(s), 2) != y))
            def _():
                pair_copy(s % 2, h).wait_send()
                cross_copy(s % 2, core, h).wait_send()

    for h in range(halves):
        @pl.when(jnp.logical_not(late_owner))
        def _():
            for d in range(1, n_z):
                d1_copy(lax.rem(z + d, n_z), z, h).wait_send()

        @pl.when(late_root)
        def _():
            for to in range(n_z):
                late_d1(to, h).wait_send()

        for d in range(1, n_z * n_x):
            d2_copy(lax.rem(c + d, n_z * n_x), c, h).wait_send()
        for w in range(2):
            sel_copy(w, h).wait()
    diag_copy.wait()


def fused(n_prow, n_pcol, ainv, lpanel, dinv, rowblocks, counts, widths):
    n_z, n_x = n_prow, 2
    rows, depth = ainv.shape
    bf, f32, H = jnp.bfloat16, jnp.float32, 128
    halves = B // H
    hbm = pl.BlockSpec(memory_space=pltpu.HBM)
    dma = pltpu.SemaphoreType.DMA
    piece = (2, halves, rows, H)
    results = pl.pallas_call(
        functools.partial(level_kernel, n_z, n_x),
        out_shape=(
            jax.ShapeDtypeStruct((rows, dinv.shape[1]), bf),
            jax.ShapeDtypeStruct(dinv.shape, f32),
        ),
        in_specs=[hbm] * 6,
        out_specs=(hbm, hbm),
        scratch_shapes=[
            pltpu.VMEM((rows, dinv.shape[1]), bf),
            pltpu.VMEM(dinv.shape, f32),
            pltpu.VMEM((2, rows, depth), bf),
            pltpu.VMEM(lpanel.shape, bf),
            pltpu.VMEM(dinv.shape, f32),
            pltpu.SMEM(rowblocks.shape, jnp.int32),
            pltpu.SMEM(counts.shape, jnp.int32),
            pltpu.SMEM(widths.shape, jnp.int32),
            pltpu.VMEM((n_z, halves, depth, H), bf),
            pltpu.VMEM((halves, depth, H), bf),
            pltpu.VMEM((B, depth), bf),
            pltpu.VMEM(piece, f32),
            pltpu.VMEM(piece, f32),
        ]
        + [pltpu.VMEM(piece, bf)] * 6
        + [
            pltpu.VMEM((depth, B), bf),
            pltpu.VMEM((halves, rows, H), bf),
            pltpu.VMEM((halves, rows, H), bf),
            pltpu.VMEM((halves, B, H), bf),
            pltpu.VMEM((n_z, halves, B // n_z, H), bf),
            pltpu.VMEM((n_z * n_x, halves, B // n_z, H), bf),
            pltpu.VMEM((halves, rows, H), f32),
            pltpu.VMEM((halves, rows, H), bf),
            pltpu.VMEM((halves, rows, H), bf),
            pltpu.VMEM((halves, rows, H), bf),
            pltpu.VMEM((2, 2, halves, rows, H), bf),
            pltpu.VMEM((halves, B, H), bf),
            dma((6,)),
            dma((2,)),
            dma((2, n_z, halves)),
            dma((n_z, halves)),
            dma((n_z, halves)),
            dma((halves,)),
        ]
        + [dma((2, halves))] * 6
        + [
            dma((halves,)),
            dma((halves,)),
            dma((n_z, halves)),
            dma((n_z, halves)),
            dma((n_z * n_x, halves)),
            dma((n_z * n_x, halves)),
            dma((halves,)),
            dma((halves,)),
            dma((2, halves)),
            dma((2, 2, halves)),
            dma((n_z, halves)),
            dma((3, halves)),
        ],
        compiler_params=pltpu.CompilerParams(
            collective_id=0, has_side_effects=True, vmem_limit_bytes=60 * 1024 * 1024
        ),
        cost_estimate=pl.CostEstimate(
            flops=2 * rows * depth * SNODES * B, bytes_accessed=4 * 1024 * 1024, transcendentals=0
        ),
    )(ainv, lpanel, dinv, rowblocks, counts, widths)
    anywhere = pl.BlockSpec(memory_space=pl.ANY)
    return pl.pallas_call(
        handoff_kernel,
        out_shape=tuple(jax.ShapeDtypeStruct(r.shape, r.dtype) for r in results),
        in_specs=[anywhere] * 2,
        out_specs=(anywhere, anywhere),
        scratch_shapes=[pltpu.VMEM(r.shape, r.dtype) for r in results]
        + [dma((2 * PIECES,)), dma((2 * PIECES,))],
        compiler_params=pltpu.CompilerParams(vmem_limit_bytes=60 * 1024 * 1024),
    )(*results)


def solution(mesh):
    n_prow, n_pcol = mesh.shape["prow"], mesh.shape["pcol"]

    def step(ainv, lpanel, dinv, rowblocks, counts, widths):
        rows, depth = ainv.shape
        whole = n_prow == 4 and n_pcol == 8 and lpanel.shape[1] == B and dinv.shape[1] == 2 * B
        if whole and depth == 2 * rows and depth == lpanel.shape[0] and rows % B == 0 and B % (16 * n_prow) == 0:
            return fused(n_prow, n_pcol, ainv, lpanel, dinv, rowblocks, counts, widths)
        return per_device(ainv, lpanel, dinv, rowblocks, counts, widths)

    placed = (P("pcol", "prow"), P("prow", "pcol"), P(None, "prow"), P(), P(), P())
    return jax.shard_map(
        step,
        mesh=mesh,
        in_specs=placed,
        out_specs=(P("pcol", "prow"), P(None, "prow")),
        check_vma=False,
    )
```
